128 devices in a mesh: dp: 8 (over x_hi, z), tensor: 16 (over y, x_lo, core).
Axes of the slice: x: 4 (x_hi: 2, x_lo: 2; x = x_hi * 2 + x_lo), y: 4, z: 4, core: 2. Of those that a mesh axis runs over, the one named last changes fastest.
Arguments:
- qkv: bfloat16 [8192, 3, 14336], P('dp', None, 'tensor'), may hold values from -16 to 16
- doc_ids: int32 [8192], P('dp'), may hold values from 0 to 47, never falling along the last dimension, each value on 1 to 256 neighbouring positions
- old_weight: bfloat16 [112, 128, 8192], P('dp', None, 'tensor'), may hold values from -0.046875 to 0.046875
- old_moment: float32 [112, 128, 8192], P('dp', None, 'tensor'), may hold values from -6 to 6
Outputs:
- new_weight: bfloat16 [112, 128, 8192], P('tensor', 'dp')
- new_moment: float32 [112, 128, 8192], P('tensor', 'dp')
- projected: bfloat16 [8192, 8192], P(('dp', 'tensor'))
The draws below stay inside these ranges and needn't reach their ends.
All inputs are finite; a program needn't handle non-finite values.
Results may differ from the reference program's by a relative error of at most 0.022.
Values may be sent and summed in bfloat16 or wider, within the bound.
No kernel may reach another device: no remote copies, remote signals or barrier semaphores. Data moves between devices by JAX's collectives and lax.ppermute only.
A program may use at most 192 MiB of HBM per device.

```python
import math
import jax
import jax.numpy as jnp
import numpy as np
from jax import lax

HEADS = 112
HEAD_DIM = 128
OUTW = 8192
SEQ = 512
D = 14336
TOKENS = 8192
N_TENSOR = 16


def draw_qkv(key, part):
    key = jax.random.fold_in(key, 11)
    key_base = jax.random.fold_in(key, 0)
    base = jax.random.normal(key_base, (TOKENS, 3, D), jnp.float32)
    return base.astype(jnp.bfloat16)


def levels(own_key, extent, pieces, least, largest):
    def one(dim, shards_of):
        heights = jax.random.uniform(jax.random.fold_in(jax.random.fold_in(own_key, 6), dim), (shards_of,), jnp.float32, least / len(pieces), largest / len(pieces))
        return jnp.repeat(jnp.exp(heights), extent[dim] // shards_of).reshape((-1,) + (1,) * (len(extent) - dim - 1))

    level = one(*pieces[0])
    for cut in pieces[1:]:
        level = level * one(*cut)
    return level


def profile(amount, total, limit, skew):
    portions = [(1 << 20) // math.isqrt(grade ** skew) + 1 for grade in range(2, amount + 1)]
    rest, holding = total - limit - (amount - 1), [1] * (amount - 1)
    while rest > 0:
        free = [i for i in range(amount - 1) if holding[i] < limit]
        pool, remaining = sum([portions[i] for i in free]), rest
        for i in free:
            addition = min(limit - holding[i], max(1, remaining * portions[i] // pool), rest)
            holding[i] = holding[i] + addition
            rest = rest - addition
    return np.array([limit] + holding)


def ragged_sizes(rng, count, total, bound, slope):
    if count == 2:
        one = jax.random.randint(rng, (), max(1, total - bound), min(bound, total - 1) + 1)
        return jnp.stack([one, total - one])
    lengths = jnp.asarray(profile(count, total, bound, slope), jnp.int32)
    pairs = (count - 1) // 2
    donor, sink = lengths[1:1 + 2 * pairs:2], lengths[2:2 + 2 * pairs:2]
    margin = jnp.minimum(donor - 1, bound - sink)
    shifted = jax.random.randint(jax.random.fold_in(rng, 1), (pairs,), 0, 1 << 20) % (margin + 1)
    lengths = lengths.at[1:1 + 2 * pairs:2].set(donor - shifted).at[2:2 + 2 * pairs:2].set(sink + shifted)
    return lengths[jax.random.permutation(jax.random.fold_in(rng, 2), count)]


def bell_draw(stream_key, shape, deviation, bound, cuts=(), kind=jnp.bfloat16):
    result = jax.random.normal(stream_key, shape, jnp.float32) * deviation
    if len(cuts) > 0:
        result = levels(stream_key, shape, cuts, -0.22, 0.18) * result
    return jnp.clip(result, min=-bound, max=bound).astype(kind)


def setup_inputs(seed: int = 0) -> dict:
    streams_of = jax.random.split(jax.random.key(seed), 5)
    qkv = draw_qkv(jax.random.fold_in(streams_of[4], 71), 0)
    doc_ids = jnp.searchsorted(jnp.cumsum(ragged_sizes(streams_of[1], TOKENS * 3 // SEQ, TOKENS, SEQ // 2, 2)), jnp.arange(TOKENS), side="right").astype(jnp.int32)
    old_weight = bell_draw(streams_of[2], (HEADS, HEAD_DIM, OUTW), D ** -0.5, 0.046875, ((0, 8), (2, 16)))
    old_moment = bell_draw(streams_of[3], (HEADS, HEAD_DIM, OUTW), 1.0, 6.0, ((0, 8), (2, 16)), jnp.float32)
    return {"qkv": qkv, "doc_ids": doc_ids, "old_weight": old_weight, "old_moment": old_moment}


def one_sequence(block, doc_row):
    queries = block[:, 0].astype(jnp.float32)
    keys_block = block[:, 1].astype(jnp.float32)
    values_block = block[:, 2].astype(jnp.float32)
    factor = 1.0 / jnp.sqrt(jnp.float32(HEAD_DIM))
    scores = jnp.einsum('qhd,khd->hqk', queries, keys_block) * factor
    position = jnp.arange(SEQ, dtype=jnp.int32)
    allowed = (doc_row[:, None] == doc_row[None, :]) & (position[:, None] >= position[None, :])
    scores = jnp.where(allowed[None], scores, jnp.float32(-1e+30))
    row_max = lax.optimization_barrier(jnp.max(scores, axis=-1, keepdims=True))
    expd = jnp.exp(scores - row_max)
    row_total = lax.optimization_barrier(jnp.sum(expd, axis=-1, keepdims=True))
    weights_bf = (expd / row_total).astype(jnp.bfloat16)
    mixed = jnp.einsum('hqk,khd->qhd', weights_bf.astype(jnp.float32), values_block)
    return mixed.astype(jnp.bfloat16)

def reference(qkv, doc_ids, old_weight, old_moment):
    blocks = TOKENS // SEQ
    seq_grid = qkv.reshape(blocks, SEQ, 3, HEADS, HEAD_DIM)
    doc_rows = doc_ids.reshape(blocks, SEQ)
    attended = lax.map(lambda seq_pair: one_sequence(seq_pair[0], seq_pair[1]), (seq_grid, doc_rows))
    attended = attended.reshape(TOKENS, HEADS, HEAD_DIM)
    group_size = HEADS // N_TENSOR

    def add_group(running, group_index):
        first = (group_index * group_size).astype(jnp.int32)
        part_in = lax.dynamic_slice_in_dim(attended, first, group_size, 1).astype(jnp.float32)
        part_w = lax.dynamic_slice_in_dim(old_weight, first, group_size, 0).astype(jnp.float32)
        term = jnp.einsum('thd,hdo->to', part_in, part_w)
        term = lax.optimization_barrier(term.astype(jnp.bfloat16)).astype(jnp.float32)
        return (running + term, None)
    running, _ = lax.scan(add_group, jnp.zeros((TOKENS, OUTW), jnp.float32), jnp.arange(N_TENSOR, dtype=jnp.int32))
    return (old_weight, old_moment, running.astype(jnp.bfloat16))
```

```python
import functools

import jax
import jax.numpy as jnp
from jax import lax
from jax.experimental import pallas as pl
from jax.experimental.pallas import tpu as pltpu
from jax.sharding import Mesh, PartitionSpec as P

HEAD_DIM = 128
SEQ = 512
HALF = SEQ // 2
AXES = ("x_hi", "z", "y", "x_lo", "core")
SIZES = (2, 4, 4, 2, 2)


def pairs_of(move):
    def flat(c):
        n = 0
        for size, value in zip(SIZES, c):
            n = n * size + value
        return n

    out = []
    for x_hi in range(2):
        for z in range(4):
            for y in range(4):
                for x_lo in range(2):
                    for core in range(2):
                        here = (x_hi, z, y, x_lo, core)
                        out.append((flat(here), flat(move(*here))))
    return out


def send(value, move):
    return lax.ppermute(value, AXES, pairs_of(move))


def spread(c1, c2):
    def move(x_hi, z, y, x_lo, core):
        return ((y >> 1) ^ c1, 2 * ((y & 1) ^ c2) + (z & 1), 2 * x_hi + (z >> 1), x_lo, core)

    return move


def x_near(x_hi, z, y, x_lo, core):
    return (x_hi, z, y, 1 - x_lo, core)


def x_far(x_hi, z, y, x_lo, core):
    return (1 - x_hi, z, y, 1 - x_lo, core)


def z_near(x_hi, z, y, x_lo, core):
    return (x_hi, z ^ 1, y, x_lo, core)


def z_far(x_hi, z, y, x_lo, core):
    return (x_hi, z ^ 3, y, x_lo, core)


def other_core(x_hi, z, y, x_lo, core):
    return (x_hi, z, y, x_lo, 1 - core)


def y_step(k):
    return lambda x_hi, z, y, x_lo, core: (x_hi, z, (y + k) % 4, x_lo, core)


def gather4(own, near, far):
    half = own.shape[0] // 2
    from_near = send(own, near)
    from_far = send(own, far)
    first = send(from_far[:half], near)
    second = send(from_near[half:], far)
    return own, from_near, from_far, jnp.concatenate([first, second], axis=0)


def attention_kernel(row_doc, col_doc, q_ref, k_ref, v_ref, out_ref, bias):
    @pl.when(pl.program_id(1) == 0)
    def _():
        row = lax.broadcasted_iota(jnp.int32, (SEQ, SEQ), 0)
        col = lax.broadcasted_iota(jnp.int32, (SEQ, SEQ), 1)
        allowed = (row_doc[...] == col_doc[0]) & (row >= col)
        bias[...] = jnp.where(allowed, jnp.float32(0), jnp.float32(-1e30))

    factor = jnp.float32(HEAD_DIM**-0.5)
    for part in range(2):
        rows = slice(part * HALF, (part + 1) * HALF)
        keys = slice(0, (part + 1) * HALF)
        scores = lax.dot_general(
            q_ref[rows, :], k_ref[keys, :], (((1,), (1,)), ((), ())),
            preferred_element_type=jnp.float32,
        )
        scores = scores * factor + bias[rows, keys]
        top = jnp.max(scores, axis=-1, keepdims=True)
        expd = jnp.exp(scores - top)
        total = jnp.sum(expd, axis=-1, keepdims=True)
        mixed = jnp.dot(
            expd.astype(jnp.bfloat16), v_ref[keys, :], preferred_element_type=jnp.float32
        )
        out_ref[rows, :] = (mixed / total).astype(jnp.bfloat16)


def attention(qkv, doc_ids):
    tokens, _, width = qkv.shape
    heads = width // HEAD_DIM
    blocks = tokens // SEQ
    flat = qkv.reshape(tokens, 3 * width)

    def part(n):
        return pl.BlockSpec((SEQ, HEAD_DIM), lambda s, h: (s, n * heads + h))

    return pl.pallas_call(
        attention_kernel,
        grid=(blocks, heads),
        in_specs=[
            pl.BlockSpec((SEQ, 1), lambda s, h: (s, 0)),
            pl.BlockSpec((1, 1, SEQ), lambda s, h: (s, 0, 0)),
            part(0), part(1), part(2),
        ],
        out_specs=pl.BlockSpec((SEQ, HEAD_DIM), lambda s, h: (s, h)),
        out_shape=jax.ShapeDtypeStruct((tokens, width), jnp.bfloat16),
        scratch_shapes=[pltpu.VMEM((SEQ, SEQ), jnp.float32)],
        compiler_params=pltpu.CompilerParams(vmem_limit_bytes=32 * 2**20),
        cost_estimate=pl.CostEstimate(
            flops=4 * tokens * SEQ * width, bytes_accessed=8 * tokens * width,
            transcendentals=tokens * SEQ * heads,
        ),
        name="attention",
    )(doc_ids.reshape(tokens, 1), doc_ids.reshape(blocks, 1, SEQ), flat, flat, flat)


def project_kernel(count, place, *refs):
    acts, weights, outs = refs[:8], refs[8:12], refs[12:]
    swap, core, z1, x_hi = place[0], place[1], place[2], place[3]
    step = pl.program_id(0)
    depth, width = acts[0].shape[1], weights[0].shape[1]

    def run(cross):
        for dt in range(2):
            for dg in range(2):
                total = None
                for dv in range(2):
                    weight = weights[2 * dg + (dv ^ cross)]
                    for side in range(2):
                        base = pl.multiple_of((core ^ side) * depth, depth)
                        term = jnp.dot(
                            acts[4 * side + 2 * dt + dv][...],
                            weight[pl.ds(base, depth), :],
                            preferred_element_type=jnp.float32,
                        )
                        total = term if total is None else total + term
                total = total.astype(jnp.bfloat16)
                columns = pl.ds(pl.multiple_of((z1 ^ dg) * width, width), width)
                for n in range(count):

                    @pl.when(step == n)
                    def _():
                        outs[n][x_hi ^ dt, :, columns] = total

    @pl.when(swap == 0)
    def _():
        run(0)

    @pl.when(swap == 1)
    def _():
        run(1)


def project(place, acts, weights, steps):
    rows, depth = acts[0].shape
    rows = rows // 4
    width = weights[0].shape[1]
    count = len(steps)

    def row_block(n, place):
        k = steps[0]
        for i in range(1, count):
            k = jnp.where(n == i, steps[i], k)
        return ((place[4] + k) % 4, 0)

    shape = (2, rows, 2 * width)
    return pl.pallas_call(
        functools.partial(project_kernel, count),
        grid_spec=pltpu.PrefetchScalarGridSpec(
            num_scalar_prefetch=1,
            grid=(count,),
            in_specs=[pl.BlockSpec((rows, depth), row_block)] * 8
            + [pl.BlockSpec(weights[0].shape, lambda n, place: (0, 0))] * 4,
            out_specs=[pl.BlockSpec(shape, lambda n, place: (0, 0, 0))] * count,
        ),
        out_shape=[jax.ShapeDtypeStruct(shape, jnp.bfloat16)] * count,
        compiler_params=pltpu.CompilerParams(vmem_limit_bytes=48 * 2**20),
        cost_estimate=pl.CostEstimate(
            flops=count * 2 * 2 * rows * 2 * width * 4 * depth,
            bytes_accessed=16 * rows * depth * count + 8 * width * weights[0].shape[0],
            transcendentals=0,
        ),
        name="project",
    )(place, *acts, *weights)


def whole_columns(parts):
    _, rows, width = parts.shape
    parts = parts.reshape(2, 2, 2, rows, 2, 2, 2, width // 8)
    outer = []
    for c1 in range(2):
        inner = []
        for c2 in range(2):
            piece = parts[:, :, :, :, :, c1, c2, :]
            if c1:
                piece = piece[::-1]
            if c2:
                piece = piece[:, :, :, :, ::-1]
            inner.append(piece)
        outer.append(jnp.stack(inner))
    full = jnp.stack(outer)
    return full.transpose(5, 2, 6, 3, 4, 0, 1, 7).reshape(rows, 8 * width)


def local(qkv, doc_ids, old_weight, old_moment):
    x_hi, z, y, x_lo, core = (lax.axis_index(a) for a in AXES)
    z1, z0 = z // 2, z % 2
    ring = ("x_hi", "x_lo", "core")
    heads, feats, cols = old_weight.shape
    quarter = cols // 4

    pieces = [
        send(old_weight[:, :, quarter * (2 * c1 + c2) : quarter * (2 * c1 + c2 + 1)], spread(c1, c2))
        for c1 in range(2)
        for c2 in range(2)
    ]
    own_weight = jnp.concatenate(pieces, axis=2).reshape(heads * feats, cols)
    w00, w01, w11, w10 = gather4(own_weight, z_near, z_far)

    attended = attention(qkv, doc_ids)
    a00, a01, a11, a10 = gather4(attended, x_near, x_far)
    mine = [a00, a01, a10, a11]
    acts = mine + [send(a, other_core) for a in mine]
    weights = [w00, w01, w10, w11]

    place = jnp.stack([x_lo ^ z0, core, z1, x_hi, y]).astype(jnp.int32)
    out2, out1 = project(place, acts, weights, (2, 1))
    out3, out0 = project(place, acts, weights, (3, 0))
    total = out0.astype(jnp.float32)
    for k, part in ((2, out2), (1, out1), (3, out3)):
        total = total + send(part, y_step(k)).astype(jnp.float32)
    total = total.astype(jnp.bfloat16)
    rows = total.shape[1] // 4
    parts = lax.all_to_all(total.reshape(8, rows, total.shape[2]), ring, 0, 0, tiled=True)
    projected = whole_columns(parts)

    def feature_rows(w):
        w = w.reshape(2, heads // 2, 2, 4, feats // 8, cols)
        return lax.dynamic_index_in_dim(w, z, 3, keepdims=False)

    kept = [feature_rows(w) for w in weights]

    def in_order(bit, a, b):
        return jnp.where(bit == 0, a, b), jnp.where(bit == 0, b, a)

    g0, g1 = in_order(z1, jnp.stack(kept[:2]), jnp.stack(kept[2:]))
    both = jnp.stack([g0, g1])
    h0, h1 = in_order(z0, both[:, 0], both[:, 1])
    both = jnp.stack([h0, h1])
    both = both.transpose(4, 0, 2, 3, 5, 1, 6).reshape(8, heads // 2 * (feats // 8), 2 * cols)
    new_weight = whole_columns(lax.all_to_all(both, ring, 0, 0, tiled=True))
    new_weight = new_weight.reshape(heads // 2, feats // 8, 16 * cols)

    new_moment = lax.all_to_all(
        lax.all_to_all(
            old_moment.astype(jnp.bfloat16), ("x_hi", "z"), split_axis=1, concat_axis=0, tiled=True
        ),
        ("y", "x_lo", "core"),
        split_axis=0,
        concat_axis=2,
        tiled=True,
    ).astype(old_moment.dtype)
    return (new_weight, new_moment, projected)


def solution(mesh):
    mesh = Mesh(mesh.devices.reshape(SIZES), AXES)
    dp, tensor = ("x_hi", "z"), ("y", "x_lo", "core")
    placed = (P(dp, None, tensor), P(dp), P(dp, None, tensor), P(dp, None, tensor))
    return jax.shard_map(
        local,
        mesh=mesh,
        in_specs=placed,
        out_specs=(P(tensor, dp, None), P(tensor, dp, None), P(dp + tensor, None)),
        check_vma=False,
    )
```

```python
import functools

import jax
import jax.numpy as jnp
from jax import lax
from jax.experimental import pallas as pl
from jax.experimental.pallas import tpu as pltpu
from jax.sharding import Mesh, PartitionSpec as P

HEAD_DIM = 128
SEQ = 512
HALF = SEQ // 2
AXES = ("x_hi", "z", "y", "x_lo", "core")
SIZES = (2, 4, 4, 2, 2)


def pairs_of(move):
    def flat(c):
        n = 0
        for size, value in zip(SIZES, c):
            n = n * size + value
        return n

    out = []
    for x_hi in range(2):
        for z in range(4):
            for y in range(4):
                for x_lo in range(2):
                    for core in range(2):
                        here = (x_hi, z, y, x_lo, core)
                        out.append((flat(here), flat(move(*here))))
    return out


def send(value, move):
    return lax.ppermute(value, AXES, pairs_of(move))


def spread(c):
    def move(x_hi, z, y, x_lo, core):
        return ((y >> 1) ^ c, 2 * ((y & 1) ^ c) + (z & 1), 2 * x_hi + (z >> 1), x_lo, core)

    return move


def x_near(x_hi, z, y, x_lo, core):
    return (x_hi, z, y, 1 - x_lo, core)


def x_far(x_hi, z, y, x_lo, core):
    return (1 - x_hi, z, y, 1 - x_lo, core)


def z_near(x_hi, z, y, x_lo, core):
    return (x_hi, z ^ 1, y, x_lo, core)


def z_far(x_hi, z, y, x_lo, core):
    return (x_hi, z ^ 3, y, x_lo, core)


def other_core(x_hi, z, y, x_lo, core):
    return (x_hi, z, y, x_lo, 1 - core)


def y_step(k):
    return lambda x_hi, z, y, x_lo, core: (x_hi, z, (y + k) % 4, x_lo, core)


def gather4(own, near, far):
    from_near = [send(p, near) for p in own]
    from_far = [send(p, far) for p in own]
    opposite = [send(from_far[0], near), send(from_near[1], far)]
    return own, from_near, from_far, opposite


def attention_kernel(row_doc, col_doc, q_ref, k_ref, v_ref, out_ref, bias):
    @pl.when(pl.program_id(0) == 0)
    def _():
        row = lax.broadcasted_iota(jnp.int32, (SEQ, SEQ), 0)
        col = lax.broadcasted_iota(jnp.int32, (SEQ, SEQ), 1)
        allowed = (row_doc[...] == col_doc[0]) & (row >= col)
        bias[...] = jnp.where(allowed, jnp.float32(0), jnp.float32(-1e30))

    factor = jnp.float32(HEAD_DIM**-0.5)
    for part in range(2):
        rows = slice(part * HALF, (part + 1) * HALF)
        keys = slice(0, (part + 1) * HALF)
        scores = lax.dot_general(
            q_ref[rows, :], k_ref[keys, :], (((1,), (1,)), ((), ())),
            preferred_element_type=jnp.float32,
        )
        scores = scores * factor + bias[rows, keys]
        top = jnp.max(scores, axis=-1, keepdims=True)
        expd = jnp.exp(scores - top)
        total = jnp.sum(expd, axis=-1, keepdims=True)
        mixed = jnp.dot(
            expd.astype(jnp.bfloat16), v_ref[keys, :], preferred_element_type=jnp.float32
        )
        out_ref[rows, :] = (mixed / total).astype(jnp.bfloat16)


def attention(planes, doc_ids, sequence):
    _, tokens, width = planes.shape
    heads = width // HEAD_DIM
    blocks = tokens // SEQ

    def part(n):
        return pl.BlockSpec((None, SEQ, HEAD_DIM), lambda h: (n, sequence, h))

    return pl.pallas_call(
        attention_kernel,
        grid=(heads,),
        in_specs=[
            pl.BlockSpec((SEQ, 1), lambda h: (sequence, 0)),
            pl.BlockSpec((1, 1, SEQ), lambda h: (sequence, 0, 0)),
            part(0), part(1), part(2),
        ],
        out_specs=pl.BlockSpec((SEQ, HEAD_DIM), lambda h: (0, h)),
        out_shape=jax.ShapeDtypeStruct((SEQ, width), jnp.bfloat16),
        scratch_shapes=[pltpu.VMEM((SEQ, SEQ), jnp.float32)],
        compiler_params=pltpu.CompilerParams(vmem_limit_bytes=32 * 2**20),
        cost_estimate=pl.CostEstimate(
            flops=8 * SEQ * SEQ * width, bytes_accessed=8 * SEQ * width,
            transcendentals=SEQ * SEQ * heads,
        ),
        name="attention",
    )(doc_ids.reshape(tokens, 1), doc_ids.reshape(blocks, 1, SEQ), planes, planes, planes)


STEPS = (2, 1, 3, 0)


def project_kernel(place, *refs):
    acts, weights, outs = refs[:16], refs[16:20], refs[20:24]
    a_buf, w_buf, a_sem, w_sem = refs[24:]
    swap, core, x_hi, y = place[0], place[1], place[2], place[3]
    rows, depth = acts[0].shape[0] // 2, acts[0].shape[1]
    width = weights[0].shape[1]

    def act_copy(n, source, base, dt, dv, side):
        return pltpu.make_async_copy(
            source.at[pl.ds(base, rows), :],
            a_buf.at[n, pl.ds(pl.multiple_of((x_hi ^ dt) * rows, rows), rows),
                     pl.ds((2 * dv + side) * depth, depth)],
            a_sem.at[n, 4 * dt + 2 * dv + side],
        )

    def weight_copy(dv, side, c):
        slot = 2 * (dv ^ swap) + side
        return pltpu.make_async_copy(
            weights[2 * dv + c].at[pl.ds(pl.multiple_of((core ^ side) * depth, depth), depth), :],
            w_buf.at[pl.ds(pl.multiple_of(slot * depth, depth), depth), pl.ds(c * width, width)],
            w_sem.at[dv, side, c],
        )

    parts = [(dt, dv, side) for dt in range(2) for dv in range(2) for side in range(2)]
    pieces = [(dv, side, c) for dv in range(2) for side in range(2) for c in range(2)]

    def start_acts(n):
        target = lax.rem(y + STEPS[n], 4)
        base = pl.multiple_of(lax.rem(target, 2) * rows, rows)
        for s in range(2):

            @pl.when(target // 2 == s)
            def _():
                for dt, dv, side in parts:
                    act_copy(n, acts[8 * side + 4 * dt + 2 * dv + s], base, dt, dv, side).start()

    for piece in pieces:
        weight_copy(*piece).start()
    for n in range(4):
        start_acts(n)
    for piece in pieces:
        weight_copy(*piece).wait()
    for n in range(4):
        for dt, dv, side in parts:
            act_copy(n, acts[0], 0, dt, dv, side).wait()
        product = jnp.dot(a_buf[n], w_buf[...], preferred_element_type=jnp.float32)
        outs[n][...] = product.astype(jnp.bfloat16).reshape(2, rows, 2 * width)


def project(place, acts, weights):
    rows, depth = acts[0].shape
    rows = rows // 2
    width = weights[0].shape[1]
    shape = (2, rows, 2 * width)
    return pl.pallas_call(
        project_kernel,
        in_specs=[pl.BlockSpec(memory_space=pltpu.SMEM)] + [pl.BlockSpec(memory_space=pl.ANY)] * 20,
        out_specs=[pl.BlockSpec(memory_space=pltpu.VMEM)] * 4,
        out_shape=[jax.ShapeDtypeStruct(shape, jnp.bfloat16)] * 4,
        scratch_shapes=[
            pltpu.VMEM((4, 2 * rows, 4 * depth), jnp.bfloat16),
            pltpu.VMEM((4 * depth, 2 * width), jnp.bfloat16),
            pltpu.SemaphoreType.DMA((4, 8)),
            pltpu.SemaphoreType.DMA((2, 2, 2)),
        ],
        compiler_params=pltpu.CompilerParams(vmem_limit_bytes=40 * 2**20),
        cost_estimate=pl.CostEstimate(
            flops=4 * 2 * 2 * rows * 2 * width * 4 * depth,
            bytes_accessed=64 * rows * depth + 16 * width * depth,
            transcendentals=0,
        ),
        name="project",
    )(place, *acts, *weights)


def pack_kernel(place, *refs):
    sources, out, sem = refs[:8], refs[8], refs[9]
    z, z0 = place[0], place[1]
    heads, feats, width = sources[0].shape
    heads, feats = heads // 2, feats // 8
    copies = []
    for dg in range(2):
        for dv in range(2):
            for c in range(2):
                for x_hi in range(2):
                    for core in range(2):
                        n = len(copies)
                        first = pl.multiple_of((4 * x_hi + z) * feats, feats)
                        copies.append(pltpu.make_async_copy(
                            sources[4 * dg + 2 * dv + c].at[
                                pl.ds(core * heads, heads), pl.ds(first, feats), :],
                            out.at[4 * x_hi + 2 * (z0 ^ dv) + core, :, :,
                                   pl.ds((2 * dg + c) * width, width)],
                            sem.at[n],
                        ))
    for copy in copies:
        copy.start()
    for copy in copies:
        copy.wait()


def pack(place, sources):
    heads, feats, width = sources[0].shape
    return pl.pallas_call(
        pack_kernel,
        in_specs=[pl.BlockSpec(memory_space=pltpu.SMEM)] + [pl.BlockSpec(memory_space=pl.ANY)] * 8,
        out_specs=pl.BlockSpec(memory_space=pl.ANY),
        out_shape=jax.ShapeDtypeStruct((8, heads // 2, feats // 8, 4 * width), jnp.bfloat16),
        scratch_shapes=[pltpu.SemaphoreType.DMA((32,))],
        cost_estimate=pl.CostEstimate(
            flops=0, bytes_accessed=4 * heads * feats * width, transcendentals=0
        ),
        name="pack",
    )(place, *sources)


def whole_columns(z1, parts):
    first = jnp.where(z1 == 0, parts[0], parts[1])
    second = jnp.where(z1 == 0, parts[1], parts[0])
    full = jnp.stack([first, second])
    rows, width = full.shape[2:-1], full.shape[-1] // 2
    full = full.reshape(2, 2, 4, -1, 2, width)
    straight = full[:, :, :, :, 0]
    crossed = full[::-1, ::-1, :, :, 1]
    full = jnp.stack([straight, crossed], axis=4)
    return full.transpose(3, 1, 0, 2, 4, 5).reshape(rows + (32 * width,))


def local(qkv, doc_ids, old_weight, old_moment):
    x_hi, z, y, x_lo, core = (lax.axis_index(a).astype(jnp.int32) for a in AXES)
    z1, z0 = z // 2, z % 2
    ring = ("x_hi", "x_lo", "core")
    heads, feats, cols = old_weight.shape
    half = cols // 2

    own_weight = [
        send(old_weight[:, :, half * c : half * (c + 1)], spread(c)) for c in range(2)
    ]
    w00, w01, w11, w10 = gather4(own_weight, z_near, z_far)

    planes = qkv.transpose(1, 0, 2)
    attended = [attention(planes, doc_ids, s) for s in range(2)]
    a00, a01, a11, a10 = gather4(attended, x_near, x_far)
    mine = a00 + a01 + a10 + a11
    acts = mine + [send(a, other_core) for a in mine]
    weights = (w00 + w01, w10 + w11)

    place = jnp.stack([x_lo ^ z0, core, x_hi, y])
    parts = []
    for dg in range(2):
        outs = project(place, acts, [w.reshape(heads * feats, half) for w in weights[dg]])
        total = outs[3].astype(jnp.float32)
        for k, part in zip(STEPS[:3], outs[:3]):
            total = total + send(part, y_step(k)).astype(jnp.float32)
        total = total.astype(jnp.bfloat16)
        rows = total.shape[1] // 4
        parts.append(
            lax.all_to_all(total.reshape(8, rows, total.shape[2]), ring, 0, 0, tiled=True)
        )
    projected = whole_columns(z1, parts)

    packed = pack(jnp.stack([z, z0]), weights[0] + weights[1])
    packed = lax.all_to_all(packed, ring, 0, 0, tiled=True)
    new_weight = whole_columns(z1, (packed[..., :cols], packed[..., cols:]))

    new_moment = lax.all_to_all(
        lax.all_to_all(
            old_moment.astype(jnp.bfloat16), ("x_hi", "z"), split_axis=1, concat_axis=0, tiled=True
        ),
        ("y", "x_lo", "core"),
        split_axis=0,
        concat_axis=2,
        tiled=True,
    ).astype(old_moment.dtype)
    return (new_weight, new_moment, projected)


def solution(mesh):
    mesh = Mesh(mesh.devices.reshape(SIZES), AXES)
    dp, tensor = ("x_hi", "z"), ("y", "x_lo", "core")
    placed = (P(dp, None, tensor), P(dp), P(dp, None, tensor), P(dp, None, tensor))
    return jax.shard_map(
        local,
        mesh=mesh,
        in_specs=placed,
        out_specs=(P(tensor, dp, None), P(tensor, dp, None), P(dp + tensor, None)),
        check_vma=False,
    )
```

```python
import functools

import jax
import jax.numpy as jnp
from jax import lax
from jax.experimental import pallas as pl
from jax.experimental.pallas import tpu as pltpu
from jax.sharding import Mesh, PartitionSpec as P

HEAD_DIM = 128
SEQ = 512
HALF = SEQ // 2
AXES = ("x_hi", "z", "y", "x_lo", "core")
SIZES = (2, 4, 4, 2, 2)


def pairs_of(move):
    def flat(c):
        n = 0
        for size, value in zip(SIZES, c):
            n = n * size + value
        return n

    out = []
    for x_hi in range(2):
        for z in range(4):
            for y in range(4):
                for x_lo in range(2):
                    for core in range(2):
                        here = (x_hi, z, y, x_lo, core)
                        out.append((flat(here), flat(move(*here))))
    return out


def send(value, move):
    return lax.ppermute(value, AXES, pairs_of(move))


def spread(cross):
    def move(x_hi, z, y, x_lo, core):
        x_hi, z, y = (y >> 1) ^ core, 2 * ((y & 1) ^ core) + (z & 1), 2 * x_hi + (z >> 1)
        return (x_hi, z, y, x_lo, core ^ cross)

    return move


def x_near(x_hi, z, y, x_lo, core):
    return (x_hi, z, y, 1 - x_lo, core)


def x_far(x_hi, z, y, x_lo, core):
    return (1 - x_hi, z, y, 1 - x_lo, core)


def x_opposite(x_hi, z, y, x_lo, core):
    return (1 - x_hi, z, y, x_lo, core)


def z_near(x_hi, z, y, x_lo, core):
    return (x_hi, z ^ 1, y, x_lo, core)


def z_far(x_hi, z, y, x_lo, core):
    return (x_hi, z ^ 3, y, x_lo, core)


def other_core(x_hi, z, y, x_lo, core):
    return (x_hi, z, y, x_lo, 1 - core)


def attention_kernel(row_doc, col_doc, q_ref, k_ref, v_ref, out_ref, bias):
    @pl.when(pl.program_id(0) == 0)
    def _():
        row = lax.broadcasted_iota(jnp.int32, (SEQ, SEQ), 0)
        col = lax.broadcasted_iota(jnp.int32, (SEQ, SEQ), 1)
        allowed = (row_doc[...] == col_doc[0]) & (row >= col)
        bias[...] = jnp.where(allowed, jnp.float32(0), jnp.float32(-1e30))

    factor = jnp.float32(HEAD_DIM**-0.5)
    for part in range(2):
        rows = slice(part * HALF, (part + 1) * HALF)
        keys = slice(0, (part + 1) * HALF)
        scores = lax.dot_general(
            q_ref[rows, :], k_ref[keys, :], (((1,), (1,)), ((), ())),
            preferred_element_type=jnp.float32,
        )
        scores = scores * factor + bias[rows, keys]
        top = jnp.max(scores, axis=-1, keepdims=True)
        expd = jnp.exp(scores - top)
        total = jnp.sum(expd, axis=-1, keepdims=True)
        mixed = jnp.dot(
            expd.astype(jnp.bfloat16), v_ref[keys, :], preferred_element_type=jnp.float32
        )
        out_ref[rows, :] = (mixed / total).astype(jnp.bfloat16)


def attention(planes, doc_ids, sequence):
    _, tokens, width = planes.shape
    heads = width // HEAD_DIM
    blocks = tokens // SEQ

    def part(n):
        return pl.BlockSpec((None, SEQ, HEAD_DIM), lambda h: (n, sequence, h))

    return pl.pallas_call(
        attention_kernel,
        grid=(heads,),
        in_specs=[
            pl.BlockSpec((SEQ, 1), lambda h: (sequence, 0)),
            pl.BlockSpec((1, 1, SEQ), lambda h: (sequence, 0, 0)),
            part(0), part(1), part(2),
        ],
        out_specs=pl.BlockSpec((SEQ, HEAD_DIM), lambda h: (0, h)),
        out_shape=jax.ShapeDtypeStruct((SEQ, width), jnp.bfloat16),
        scratch_shapes=[pltpu.VMEM((SEQ, SEQ), jnp.float32)],
        compiler_params=pltpu.CompilerParams(vmem_limit_bytes=32 * 2**20),
        cost_estimate=pl.CostEstimate(
            flops=8 * SEQ * SEQ * width, bytes_accessed=8 * SEQ * width,
            transcendentals=SEQ * SEQ * heads,
        ),
        name="attention",
    )(doc_ids.reshape(tokens, 1), doc_ids.reshape(blocks, 1, SEQ), planes, planes, planes)


def project_kernel(place, *refs):
    acts, weights, kept, other = refs[:8], refs[8:12], refs[12], refs[13]
    a_buf, w_buf, a_sem, w_sem = refs[14:]
    swap, core, x_lo = place[0], place[1], place[2]
    depth = acts[0].shape[1]
    width = weights[0].shape[1]
    rows = acts[0].shape[0] // 8
    half = 4 * rows

    def act_copy(n, source, base, dt, dv, low, side):
        first = base + (2 * (x_lo ^ low) + (core ^ side)) * rows
        target = side * half + (2 * dt + low) * rows
        return pltpu.make_async_copy(
            source.at[pl.ds(pl.multiple_of(first, rows), rows), :],
            a_buf.at[n, pl.ds(target, rows), pl.ds(dv * depth, depth)],
            a_sem.at[n, 8 * dt + 4 * dv + 2 * low + side],
        )

    def weight_copy(dv, e):
        return pltpu.make_async_copy(
            weights[2 * dv + e],
            w_buf.at[pl.ds(pl.multiple_of((dv ^ swap) * depth, depth), depth),
                     pl.ds(pl.multiple_of((core ^ e) * width, width), width)],
            w_sem.at[dv, e],
        )

    parts = [(dt, dv, low, side) for dt in range(2) for dv in range(2)
             for low in range(2) for side in range(2)]
    pieces = [(dv, e) for dv in range(2) for e in range(2)]

    for piece in pieces:
        weight_copy(*piece).start()
    for n in range(4):
        for dt, dv, low, side in parts:
            source = acts[4 * dt + 2 * dv + n // 2]
            act_copy(n, source, n % 2 * half, dt, dv, low, side).start()
    for piece in pieces:
        weight_copy(*piece).wait()
    for n in range(4):
        for dt, dv, low, side in parts:
            act_copy(n, acts[0], 0, dt, dv, low, side).wait()
        product = jnp.dot(a_buf[n], w_buf[...], preferred_element_type=jnp.float32)
        kept[n] = product[:half].astype(jnp.bfloat16)
        other[n] = product[half:].astype(jnp.bfloat16)


def project(place, acts, weights, work):
    rows, depth = acts[0].shape
    rows = rows // 2
    width = weights[0].shape[1]
    shape = (4, rows, 2 * width)
    return pl.pallas_call(
        project_kernel,
        in_specs=[pl.BlockSpec(memory_space=pltpu.SMEM)] + [pl.BlockSpec(memory_space=pl.ANY)] * 12,
        out_specs=[pl.BlockSpec(memory_space=pltpu.VMEM)] * 2,
        out_shape=[
            jax.ShapeDtypeStruct(shape, jnp.bfloat16),
            jax.ShapeDtypeStruct(shape, jnp.bfloat16),
        ],
        scratch_shapes=[
            pltpu.VMEM((4, 2 * rows, 2 * depth), jnp.bfloat16),
            pltpu.VMEM((2 * depth, 2 * width), jnp.bfloat16),
            pltpu.SemaphoreType.DMA((4, 16)),
            pltpu.SemaphoreType.DMA((2, 2)),
        ],
        compiler_params=pltpu.CompilerParams(vmem_limit_bytes=56 * 2**20),
        cost_estimate=pl.CostEstimate(
            flops=work, bytes_accessed=1, transcendentals=0
        ),
        name="project",
    )(place, *acts, *weights)


def pack_kernel(place, *refs):
    sources, outs = refs[:16], refs[16:]
    cross, core = place[2], place[3]
    width = sources[0].shape[2]

    def run(cross):
        for dx in range(2):
            for dg in range(2):
                for dv in range(2):
                    for e in range(2):
                        column = pl.multiple_of((2 * dg + (core ^ e)) * width, width)
                        outs[2 * dx + (dv ^ cross)][:, :, pl.ds(column, width)] = sources[
                            8 * dx + 4 * dg + 2 * dv + e
                        ][...]

    for n in range(2):

        @pl.when(cross == n)
        def _():
            run(n)


def pack(place, sources):
    heads, feats, width = sources[0].shape
    share = feats // 8

    def part(dx):
        return pl.BlockSpec(
            (heads, share, width), lambda n, place: (0, 4 * (place[1] ^ dx) + place[0], 0)
        )

    shape = (heads, share, 4 * width)
    return pl.pallas_call(
        pack_kernel,
        grid_spec=pltpu.PrefetchScalarGridSpec(
            num_scalar_prefetch=1,
            grid=(1,),
            in_specs=[part(0)] * 8 + [part(1)] * 8,
            out_specs=[pl.BlockSpec(shape, lambda n, place: (0, 0, 0))] * 4,
        ),
        out_shape=[jax.ShapeDtypeStruct(shape, jnp.bfloat16)] * 4,
        compiler_params=pltpu.CompilerParams(vmem_limit_bytes=56 * 2**20),
        cost_estimate=pl.CostEstimate(
            flops=0, bytes_accessed=4 * heads * feats * width, transcendentals=0
        ),
        name="pack",
    )(place, *sources, *sources)


def columns_kernel(place, *refs):
    sources, out = refs[:8], refs[8]
    x_hi, x_lo, z1 = place[0], place[1], place[2]
    width = sources[0].shape[1] // 2
    for dg in range(2):
        for dx in range(2):
            for dl in range(2):
                for p in range(2):
                    y1, y0 = x_hi ^ (dx ^ p), z1 ^ (dg ^ p)
                    column = 8 * y1 + 4 * y0 + 2 * (x_lo ^ dl) + p
                    column = pl.multiple_of(column * width, width)
                    out[:, pl.ds(column, width)] = sources[4 * dg + 2 * dx + dl][
                        :, p * width : (p + 1) * width
                    ]


def whole_columns(place, first, second, at):
    rows, width = first[0].shape[0], 1024

    def part(n):
        return pl.BlockSpec((rows, width), lambda r, place: (0, n))

    return pl.pallas_call(
        columns_kernel,
        grid_spec=pltpu.PrefetchScalarGridSpec(
            num_scalar_prefetch=1,
            grid=(1,),
            in_specs=[part(at[0])] * 4 + [part(at[1])] * 4,
            out_specs=pl.BlockSpec((rows, 8 * width), lambda r, place: (0, 0)),
        ),
        out_shape=jax.ShapeDtypeStruct((rows, 8 * width), jnp.bfloat16),
        compiler_params=pltpu.CompilerParams(vmem_limit_bytes=56 * 2**20),
        cost_estimate=pl.CostEstimate(
            flops=0, bytes_accessed=32 * rows * width, transcendentals=0
        ),
        name="columns",
    )(place, *first, *second)


def exchange(own, near, opposite, far):
    return [own, send(near, x_near), send(opposite, x_opposite), send(far, x_far)]


def moment_kernel(parts, out):
    count, _, _, cols = parts.shape
    for n in range(count):
        out[:, :, n * cols : (n + 1) * cols] = parts[n].astype(jnp.float32)


def moment_columns(parts):
    count, heads, feats, cols = parts.shape
    step = 4
    return pl.pallas_call(
        moment_kernel,
        grid=(count // step,),
        in_specs=[pl.BlockSpec((step, heads, feats, cols), lambda n: (n, 0, 0, 0))],
        out_specs=pl.BlockSpec((heads, feats, step * cols), lambda n: (0, 0, n)),
        out_shape=jax.ShapeDtypeStruct((heads, feats, count * cols), jnp.float32),
        compiler_params=pltpu.CompilerParams(vmem_limit_bytes=56 * 2**20),
        cost_estimate=pl.CostEstimate(
            flops=0, bytes_accessed=6 * parts.size, transcendentals=0
        ),
        name="moment_columns",
    )(parts)


def tie(*values):
    return lax.optimization_barrier(values)


def local(qkv, doc_ids, old_weight, old_moment):
    x_hi, z, y, x_lo, core = (lax.axis_index(a).astype(jnp.int32) for a in AXES)
    z1, z0 = z // 2, z % 2
    ring = ("x_hi", "x_lo")
    heads, feats, cols = old_weight.shape
    heads = heads // 2

    w0 = send(lax.dynamic_slice_in_dim(old_weight, core * heads, heads, 0), spread(0))
    w1 = send(lax.dynamic_slice_in_dim(old_weight, (1 - core) * heads, heads, 0), spread(1))
    planes = qkv.transpose(1, 0, 2)
    a0 = attention(planes, doc_ids, 0)
    a1 = attention(planes, doc_ids, 1)
    near_a0, far_a0 = send(a0, x_near), send(a0, x_far)
    w0, w1, a1, near_a0, far_a0 = tie(w0, w1, a1, near_a0, far_a0)
    near_a1, far_a1 = send(a1, x_near), send(a1, x_far)
    near_w0, far_w0 = send(w0, z_near), send(w0, z_far)
    near_w0, far_w0, near_a1, far_a1, far_a0, w1 = tie(near_w0, far_w0, near_a1, far_a1, far_a0, w1)
    opp_a0, opp_a1 = send(far_a0, x_near), send(near_a1, x_far)
    near_w1, far_w1 = send(w1, z_near), send(w1, z_far)
    near_w1, far_w1, far_w0, opp_a0, opp_a1, old_moment = tie(
        near_w1, far_w1, far_w0, opp_a0, opp_a1, old_moment
    )
    opp_w0, opp_w1 = send(far_w0, z_near), send(near_w1, z_far)
    moment = old_moment.astype(jnp.bfloat16).reshape(2 * heads, 8, feats // 8, cols)
    moment = moment.transpose(1, 0, 2, 3)
    moment = lax.all_to_all(moment, ("x_hi", "z"), 0, 0, tiled=True)

    acts = [a0, a1, near_a0, near_a1, opp_a0, opp_a1, far_a0, far_a1]
    weights = ([w0, w1, near_w0, near_w1], [opp_w0, opp_w1, far_w0, far_w1])
    place = jnp.stack([x_lo ^ z0, core, x_lo])
    parts = []
    for dg in range(2):
        kept, other = project(place, acts, [w.reshape(heads * feats, cols) for w in weights[dg]],
                              (1, 1)[dg])
        if dg == 0:
            other, opp_w0, opp_w1 = tie(other, opp_w0, opp_w1)
            weights = (weights[0], [opp_w0, opp_w1, far_w0, far_w1])
        else:
            other, moment = tie(other, moment)
            moment = moment.reshape(16, heads, feats // 8, cols)
            moment = lax.all_to_all(moment, ("y", "x_lo", "core"), 0, 0, tiled=True)
            kept, *packed = tie(kept, *weights[0], *weights[1])
        total = kept.astype(jnp.float32) + send(other, other_core).astype(jnp.float32)
        total = total.astype(jnp.bfloat16)
        if dg == 0:
            place, _ = tie(place, total)
        total = lax.psum_scatter(total, "y", scatter_dimension=0, tiled=True)
        if dg == 1:
            total, moment = tie(total, moment)
        total = total.reshape(4, total.shape[1] // 4, total.shape[2])
        parts.append(exchange(*[total[n] for n in range(4)]))
    columns_place = jnp.stack([x_hi, x_lo, z1])
    projected = whole_columns(columns_place, parts[0], parts[1], (0, 0))

    packed = exchange(*pack(jnp.stack([z, x_hi, z0 ^ x_lo, core]), packed))
    packed = [p.reshape(heads * (feats // 8), 4 * cols) for p in packed]
    new_weight = whole_columns(columns_place, packed, packed, (0, 1))
    new_weight = new_weight.reshape(heads, feats // 8, 16 * cols)
    return (new_weight, moment_columns(moment), projected)


def solution(mesh):
    mesh = Mesh(mesh.devices.reshape(SIZES), AXES)
    dp, tensor = ("x_hi", "z"), ("y", "x_lo", "core")
    placed = (P(dp, None, tensor), P(dp), P(dp, None, tensor), P(dp, None, tensor))
    return jax.shard_map(
        local,
        mesh=mesh,
        in_specs=placed,
        out_specs=(P(tensor, dp, None), P(tensor, dp, None), P(dp + tensor, None)),
        check_vma=False,
    )
```

```python
import functools

import jax
import jax.numpy as jnp
from jax import lax
from jax.experimental import pallas as pl
from jax.experimental.pallas import tpu as pltpu
from jax.sharding import Mesh, PartitionSpec as P

HEAD_DIM = 128
SEQ = 512
HALF = SEQ // 2
AXES = ("x_hi", "z", "y", "x_lo", "core")
SIZES = (2, 4, 4, 2, 2)


def pairs_of(move):
    def flat(c):
        n = 0
        for size, value in zip(SIZES, c):
            n = n * size + value
        return n

    out = []
    for x_hi in range(2):
        for z in range(4):
            for y in range(4):
                for x_lo in range(2):
                    for core in range(2):
                        here = (x_hi, z, y, x_lo, core)
                        out.append((flat(here), flat(move(*here))))
    return out


def send(value, move):
    return lax.ppermute(value, AXES, pairs_of(move))


def spread(cross):
    def move(x_hi, z, y, x_lo, core):
        x_hi, z, y = (y >> 1) ^ core, 2 * ((y & 1) ^ core) + (z & 1), 2 * x_hi + (z >> 1)
        return (x_hi, z, y, x_lo, core ^ cross)

    return move


def x_near(x_hi, z, y, x_lo, core):
    return (x_hi, z, y, 1 - x_lo, core)


def x_far(x_hi, z, y, x_lo, core):
    return (1 - x_hi, z, y, 1 - x_lo, core)


def x_opposite(x_hi, z, y, x_lo, core):
    return (1 - x_hi, z, y, x_lo, core)


def z_near(x_hi, z, y, x_lo, core):
    return (x_hi, z ^ 1, y, x_lo, core)


def z_far(x_hi, z, y, x_lo, core):
    return (x_hi, z ^ 3, y, x_lo, core)


def other_core(x_hi, z, y, x_lo, core):
    return (x_hi, z, y, x_lo, 1 - core)


def y_step(k):
    return lambda x_hi, z, y, x_lo, core: (x_hi, z, (y + k) % 4, x_lo, core)


def attention_kernel(row_doc, col_doc, q_ref, k_ref, v_ref, out_ref, bias):
    @pl.when(pl.program_id(0) == 0)
    def _():
        row = lax.broadcasted_iota(jnp.int32, (SEQ, SEQ), 0)
        col = lax.broadcasted_iota(jnp.int32, (SEQ, SEQ), 1)
        allowed = (row_doc[...] == col_doc[0]) & (row >= col)
        bias[...] = jnp.where(allowed, jnp.float32(0), jnp.float32(-1e30))

    factor = jnp.float32(HEAD_DIM**-0.5)
    for part in range(2):
        rows = slice(part * HALF, (part + 1) * HALF)
        keys = slice(0, (part + 1) * HALF)
        scores = lax.dot_general(
            q_ref[rows, :], k_ref[keys, :], (((1,), (1,)), ((), ())),
            preferred_element_type=jnp.float32,
        )
        scores = scores * factor + bias[rows, keys]
        top = jnp.max(scores, axis=-1, keepdims=True)
        expd = jnp.exp(scores - top)
        total = jnp.sum(expd, axis=-1, keepdims=True)
        mixed = jnp.dot(
            expd.astype(jnp.bfloat16), v_ref[keys, :], preferred_element_type=jnp.float32
        )
        out_ref[rows, :] = (mixed / total).astype(jnp.bfloat16)


def attention(planes, doc_ids, sequence):
    _, tokens, width = planes.shape
    heads = width // HEAD_DIM
    blocks = tokens // SEQ

    def part(n):
        return pl.BlockSpec((None, SEQ, HEAD_DIM), lambda h: (n, sequence, h))

    return pl.pallas_call(
        attention_kernel,
        grid=(heads,),
        in_specs=[
            pl.BlockSpec((SEQ, 1), lambda h: (sequence, 0)),
            pl.BlockSpec((1, 1, SEQ), lambda h: (sequence, 0, 0)),
            part(0), part(1), part(2),
        ],
        out_specs=pl.BlockSpec((SEQ, HEAD_DIM), lambda h: (0, h)),
        out_shape=jax.ShapeDtypeStruct((SEQ, width), jnp.bfloat16),
        scratch_shapes=[pltpu.VMEM((SEQ, SEQ), jnp.float32)],
        compiler_params=pltpu.CompilerParams(vmem_limit_bytes=32 * 2**20),
        cost_estimate=pl.CostEstimate(
            flops=8 * SEQ * SEQ * width, bytes_accessed=8 * SEQ * width,
            transcendentals=SEQ * SEQ * heads,
        ),
        name="attention",
    )(doc_ids.reshape(tokens, 1), doc_ids.reshape(blocks, 1, SEQ), planes, planes, planes)


STEPS = (2, 1, 3, 0)


def project_kernel(place, *refs):
    acts, weights, kept, other = refs[:8], refs[8:12], refs[12], refs[13]
    a_buf, w_buf, o_buf, a_sem, w_sem, o_sem = refs[14:]
    swap, core, x_lo, y = place[0], place[1], place[2], place[3]
    depth = acts[0].shape[1]
    width = weights[0].shape[1]
    rows = acts[0].shape[0] // 8
    half = 4 * rows

    def act_copy(n, source, base, dt, dv, low, side):
        first = base + (2 * (x_lo ^ low) + (core ^ side)) * rows
        target = side * half + (2 * dt + low) * rows
        return pltpu.make_async_copy(
            source.at[pl.ds(pl.multiple_of(first, rows), rows), :],
            a_buf.at[n, pl.ds(target, rows), pl.ds(dv * depth, depth)],
            a_sem.at[n, 8 * dt + 4 * dv + 2 * low + side],
        )

    def weight_copy(dv, e):
        return pltpu.make_async_copy(
            weights[2 * dv + e],
            w_buf.at[pl.ds(pl.multiple_of((dv ^ swap) * depth, depth), depth),
                     pl.ds(pl.multiple_of((core ^ e) * width, width), width)],
            w_sem.at[dv, e],
        )

    parts = [(dt, dv, low, side) for dt in range(2) for dv in range(2)
             for low in range(2) for side in range(2)]
    pieces = [(dv, e) for dv in range(2) for e in range(2)]

    def start_acts(n):
        target = lax.rem(y + STEPS[n], 4)
        base = lax.rem(target, 2) * half
        for s in range(2):

            @pl.when(target // 2 == s)
            def _():
                for dt, dv, low, side in parts:
                    act_copy(n, acts[4 * dt + 2 * dv + s], base, dt, dv, low, side).start()

    start_acts(0)
    for piece in pieces:
        weight_copy(*piece).start()
    for piece in pieces:
        weight_copy(*piece).wait()
    for n in range(1, 4):
        start_acts(n)
    out_copies = []
    for n in range(4):
        for dt, dv, low, side in parts:
            act_copy(n, acts[0], 0, dt, dv, low, side).wait()
        for side, out in ((1, other), (0, kept)):
            product = jnp.dot(
                a_buf[n, side * half : (side + 1) * half], w_buf[...],
                preferred_element_type=jnp.float32,
            )
            o_buf[n, side] = product.astype(jnp.bfloat16)
            copy = pltpu.make_async_copy(o_buf.at[n, side], out.at[n], o_sem.at[n, side])
            copy.start()
            out_copies.append(copy)
    for copy in out_copies:
        copy.wait()


def project(place, acts, weights, work):
    rows, depth = acts[0].shape
    rows = rows // 2
    width = weights[0].shape[1]
    shape = (4, rows, 2 * width)
    return pl.pallas_call(
        project_kernel,
        in_specs=[pl.BlockSpec(memory_space=pltpu.SMEM)] + [pl.BlockSpec(memory_space=pl.ANY)] * 12,
        out_specs=[pl.BlockSpec(memory_space=pl.ANY)] * 2,
        out_shape=[
            jax.ShapeDtypeStruct(shape, jnp.bfloat16),
            jax.ShapeDtypeStruct(shape, jnp.bfloat16),
        ],
        scratch_shapes=[
            pltpu.VMEM((4, 2 * rows, 2 * depth), jnp.bfloat16),
            pltpu.VMEM((2 * depth, 2 * width), jnp.bfloat16),
            pltpu.VMEM((4, 2, rows, 2 * width), jnp.bfloat16),
            pltpu.SemaphoreType.DMA((4, 16)),
            pltpu.SemaphoreType.DMA((2, 2)),
            pltpu.SemaphoreType.DMA((4, 2)),
        ],
        compiler_params=pltpu.CompilerParams(vmem_limit_bytes=56 * 2**20),
        cost_estimate=pl.CostEstimate(
            flops=work, bytes_accessed=1, transcendentals=0
        ),
        name="project",
    )(place, *acts, *weights)


def pack_kernel(place, *refs):
    sources, out = refs[:8], refs[8]
    z0, core = place[1], place[2]
    width = sources[0].shape[2]
    for dg in range(2):
        for dv in range(2):
            for e in range(2):
                column = pl.multiple_of((2 * dg + (core ^ e)) * width, width)
                out[z0 ^ dv, :, :, pl.ds(column, width)] = sources[4 * dg + 2 * dv + e][...]


def pack(place, sources):
    heads, feats, width = sources[0].shape
    share = feats // 8
    return pl.pallas_call(
        pack_kernel,
        grid_spec=pltpu.PrefetchScalarGridSpec(
            num_scalar_prefetch=1,
            grid=(2,),
            in_specs=[pl.BlockSpec((heads, share, width), lambda n, place: (0, 4 * n + place[0], 0))] * 8,
            out_specs=pl.BlockSpec((2, heads, share, 4 * width), lambda n, place: (n, 0, 0, 0)),
        ),
        out_shape=jax.ShapeDtypeStruct((4, heads, share, 4 * width), jnp.bfloat16),
        compiler_params=pltpu.CompilerParams(vmem_limit_bytes=56 * 2**20),
        cost_estimate=pl.CostEstimate(
            flops=0, bytes_accessed=4 * heads * feats * width, transcendentals=0
        ),
        name="pack",
    )(place, *sources)


def columns_kernel(place, *refs):
    sources, out = refs[:8], refs[8]
    x_hi, x_lo, z1 = place[0], place[1], place[2]
    width = sources[0].shape[1] // 2
    for dg in range(2):
        for dx in range(2):
            for dl in range(2):
                for p in range(2):
                    y1, y0 = x_hi ^ (dx ^ p), z1 ^ (dg ^ p)
                    column = 8 * y1 + 4 * y0 + 2 * (x_lo ^ dl) + p
                    column = pl.multiple_of(column * width, width)
                    out[:, pl.ds(column, width)] = sources[4 * dg + 2 * dx + dl][
                        :, p * width : (p + 1) * width
                    ]


def whole_columns(place, sources, specs):
    rows, width = specs[0].block_shape[-2:]
    return pl.pallas_call(
        columns_kernel,
        grid_spec=pltpu.PrefetchScalarGridSpec(
            num_scalar_prefetch=1,
            grid=(1,),
            in_specs=specs,
            out_specs=pl.BlockSpec((rows, 8 * width), lambda r, place: (0, 0)),
        ),
        out_shape=jax.ShapeDtypeStruct((rows, 8 * width), jnp.bfloat16),
        compiler_params=pltpu.CompilerParams(vmem_limit_bytes=56 * 2**20),
        cost_estimate=pl.CostEstimate(
            flops=0, bytes_accessed=32 * rows * width, transcendentals=0
        ),
        name="columns",
    )(place, *sources)


def exchange(own, near, opposite, far):
    return [own, send(near, x_near), send(opposite, x_opposite), send(far, x_far)]


def moment_kernel(parts, out):
    count, _, _, cols = parts.shape
    for n in range(count):
        out[:, :, n * cols : (n + 1) * cols] = parts[n].astype(jnp.float32)


def moment_columns(parts):
    count, heads, feats, cols = parts.shape
    step = 4
    return pl.pallas_call(
        moment_kernel,
        grid=(count // step,),
        in_specs=[pl.BlockSpec((step, heads, feats, cols), lambda n: (n, 0, 0, 0))],
        out_specs=pl.BlockSpec((heads, feats, step * cols), lambda n: (0, 0, n)),
        out_shape=jax.ShapeDtypeStruct((heads, feats, count * cols), jnp.float32),
        compiler_params=pltpu.CompilerParams(vmem_limit_bytes=56 * 2**20),
        cost_estimate=pl.CostEstimate(
            flops=0, bytes_accessed=6 * parts.size, transcendentals=0
        ),
        name="moment_columns",
    )(parts)


def shares(total):
    total = total.reshape(4, total.shape[0] // 4, total.shape[1])
    return exchange(*[total[n] for n in range(4)])


def add_up(total, arrived):
    for part in arrived:
        total = total + part.astype(jnp.float32)
    return total.astype(jnp.bfloat16)


def tie(*values):
    return lax.optimization_barrier(values)


def local(qkv, doc_ids, old_weight, old_moment):
    x_hi, z, y, x_lo, core = (lax.axis_index(a).astype(jnp.int32) for a in AXES)
    z1, z0 = z // 2, z % 2
    ring = ("x_hi", "x_lo")
    heads, feats, cols = old_weight.shape
    heads = heads // 2

    w0 = send(lax.dynamic_slice_in_dim(old_weight, core * heads, heads, 0), spread(0))
    w1 = send(lax.dynamic_slice_in_dim(old_weight, (1 - core) * heads, heads, 0), spread(1))
    planes = qkv.transpose(1, 0, 2)
    a0 = attention(planes, doc_ids, 0)
    planes, w0, w1 = tie(planes, w0, w1)
    a1 = attention(planes, doc_ids, 1)
    near_a0, far_a0 = send(a0, x_near), send(a0, x_far)
    w0, w1, a1, near_a0, far_a0 = tie(w0, w1, a1, near_a0, far_a0)
    near_a1, far_a1 = send(a1, x_near), send(a1, x_far)
    near_w0, far_w0 = send(w0, z_near), send(w0, z_far)
    near_w0, far_w0, near_a1, far_a1, far_a0, w1 = tie(near_w0, far_w0, near_a1, far_a1, far_a0, w1)
    opp_a0, opp_a1 = send(far_a0, x_near), send(near_a1, x_far)
    near_w1, far_w1 = send(w1, z_near), send(w1, z_far)
    near_w1, far_w1, far_w0, opp_a0, opp_a1, old_moment = tie(
        near_w1, far_w1, far_w0, opp_a0, opp_a1, old_moment
    )
    opp_w0, opp_w1 = send(far_w0, z_near), send(near_w1, z_far)
    moment = old_moment.astype(jnp.bfloat16).reshape(2 * heads, 8, feats // 8, cols)
    opp_a0, opp_a1, moment = tie(opp_a0, opp_a1, moment.transpose(1, 0, 2, 3))
    moment = lax.all_to_all(moment, ("x_hi", "z"), 0, 0, tiled=True)

    acts = [a0, a1, near_a0, near_a1, opp_a0, opp_a1, far_a0, far_a1]
    weights = ([w0, w1, near_w0, near_w1], [opp_w0, opp_w1, far_w0, far_w1])
    place = jnp.stack([x_lo ^ z0, core, x_lo, y])
    for dg in range(2):
        kept, other = project(place, acts, [w.reshape(heads * feats, cols) for w in weights[dg]],
                              (1, 1)[dg])
        if dg == 0:
            other, opp_w0, opp_w1 = tie(other, opp_w0, opp_w1)
            weights = (weights[0], [opp_w0, opp_w1, far_w0, far_w1])
        else:
            kept, *packed = tie(kept, *weights[0], *weights[1])
            packed = pack(jnp.stack([z, z0, core]), packed)
            other, moment, arrived, packed = tie(other, moment, arrived, packed)
            first = add_up(total, arrived)
            packed = lax.all_to_all(packed, ("x_hi", "x_lo"), 0, 0, tiled=True)
        swapped = send(other, other_core)
        leave = [
            (kept[n].astype(jnp.float32) + swapped[n].astype(jnp.float32)).astype(jnp.bfloat16)
            for n in range(3)
        ]
        if dg == 0:
            place, *leave = tie(place, *leave)
        arrived = [send(leave[n], y_step(STEPS[n])) for n in range(3)]
        if dg == 1:
            moment, packed, arrived = tie(moment, packed, arrived)
            moment = moment.reshape(16, heads, feats // 8, cols)
            moment = lax.all_to_all(moment, ("y", "x_lo", "core"), 0, 0, tiled=True)
        total = kept[3].astype(jnp.float32) + swapped[3].astype(jnp.float32)
    total = add_up(total, arrived)
    total = jnp.stack([first, total])
    total = total.reshape(2, 4, total.shape[1] // 4, total.shape[2]).transpose(1, 0, 2, 3)
    parts = exchange(*[total[n] for n in range(4)])
    parts[1], moment = tie(parts[1], moment)
    rows, width = parts[0].shape[1:]
    specs = [
        pl.BlockSpec((None, rows, width), lambda r, place, dg=dg: (dg, 0, 0))
        for dg in range(2) for n in range(4)
    ]
    projected = whole_columns(jnp.stack([x_hi, x_lo, z1]), parts * 2, specs)

    packed = packed.reshape(4, heads * (feats // 8), 4 * cols)
    specs = [
        pl.BlockSpec((None, packed.shape[1], width), lambda r, place, dg=dg, n=n: (n, 0, dg))
        for dg in range(2) for n in range(4)
    ]
    new_weight = whole_columns(jnp.stack([0 * z1, 0 * z1, z1]), [packed] * 8, specs)
    new_weight = new_weight.reshape(heads, feats // 8, 16 * cols)
    return (new_weight, moment_columns(moment), projected)


def solution(mesh):
    mesh = Mesh(mesh.devices.reshape(SIZES), AXES)
    dp, tensor = ("x_hi", "z"), ("y", "x_lo", "core")
    placed = (P(dp, None, tensor), P(dp), P(dp, None, tensor), P(dp, None, tensor))
    return jax.shard_map(
        local,
        mesh=mesh,
        in_specs=placed,
        out_specs=(P(tensor, dp, None), P(tensor, dp, None), P(dp + tensor, None)),
        check_vma=False,
    )
```

```python
import functools

import jax
import jax.numpy as jnp
from jax import lax
from jax.experimental import pallas as pl
from jax.experimental.pallas import tpu as pltpu
from jax.sharding import Mesh, PartitionSpec as P

HEAD_DIM = 128
SEQ = 512
HALF = SEQ // 2
AXES = ("x_hi", "z", "y", "x_lo", "core")
SIZES = (2, 4, 4, 2, 2)


def pairs_of(move):
    def flat(c):
        n = 0
        for size, value in zip(SIZES, c):
            n = n * size + value
        return n

    out = []
    for x_hi in range(2):
        for z in range(4):
            for y in range(4):
                for x_lo in range(2):
                    for core in range(2):
                        here = (x_hi, z, y, x_lo, core)
                        out.append((flat(here), flat(move(*here))))
    return out


def send(value, move):
    return lax.ppermute(value, AXES, pairs_of(move))


def spread(cross):
    def move(x_hi, z, y, x_lo, core):
        x_hi, z, y = (y >> 1) ^ core, 2 * ((y & 1) ^ core) + (z & 1), 2 * x_hi + (z >> 1)
        return (x_hi, z, y, x_lo, core ^ cross)

    return move


def x_near(x_hi, z, y, x_lo, core):
    return (x_hi, z, y, 1 - x_lo, core)


def x_far(x_hi, z, y, x_lo, core):
    return (1 - x_hi, z, y, 1 - x_lo, core)


def x_opposite(x_hi, z, y, x_lo, core):
    return (1 - x_hi, z, y, x_lo, core)


def z_near(x_hi, z, y, x_lo, core):
    return (x_hi, z ^ 1, y, x_lo, core)


def z_far(x_hi, z, y, x_lo, core):
    return (x_hi, z ^ 3, y, x_lo, core)


def other_core(x_hi, z, y, x_lo, core):
    return (x_hi, z, y, x_lo, 1 - core)


def y_step(k):
    return lambda x_hi, z, y, x_lo, core: (x_hi, z, (y + k) % 4, x_lo, core)


def attention_kernel(row_doc, col_doc, q_ref, k_ref, v_ref, out_ref, bias):
    @pl.when(pl.program_id(0) == 0)
    def _():
        row = lax.broadcasted_iota(jnp.int32, (SEQ, SEQ), 0)
        col = lax.broadcasted_iota(jnp.int32, (SEQ, SEQ), 1)
        allowed = (row_doc[...] == col_doc[0]) & (row >= col)
        bias[...] = jnp.where(allowed, jnp.float32(0), jnp.float32(-1e30))

    factor = jnp.float32(HEAD_DIM**-0.5)
    for part in range(2):
        rows = slice(part * HALF, (part + 1) * HALF)
        keys = slice(0, (part + 1) * HALF)
        scores = lax.dot_general(
            q_ref[rows, :], k_ref[keys, :], (((1,), (1,)), ((), ())),
            preferred_element_type=jnp.float32,
        )
        scores = scores * factor + bias[rows, keys]
        top = jnp.max(scores, axis=-1, keepdims=True)
        expd = jnp.exp(scores - top)
        total = jnp.sum(expd, axis=-1, keepdims=True)
        mixed = jnp.dot(
            expd.astype(jnp.bfloat16), v_ref[keys, :], preferred_element_type=jnp.float32
        )
        out_ref[rows, :] = (mixed / total).astype(jnp.bfloat16)


def attention(planes, doc_ids, sequence):
    _, tokens, width = planes.shape
    heads = width // HEAD_DIM
    blocks = tokens // SEQ

    def part(n):
        return pl.BlockSpec((None, SEQ, HEAD_DIM), lambda h: (n, sequence, h))

    return pl.pallas_call(
        attention_kernel,
        grid=(heads,),
        in_specs=[
            pl.BlockSpec((SEQ, 1), lambda h: (sequence, 0)),
            pl.BlockSpec((1, 1, SEQ), lambda h: (sequence, 0, 0)),
            part(0), part(1), part(2),
        ],
        out_specs=pl.BlockSpec((SEQ, HEAD_DIM), lambda h: (0, h)),
        out_shape=jax.ShapeDtypeStruct((SEQ, width), jnp.bfloat16),
        scratch_shapes=[pltpu.VMEM((SEQ, SEQ), jnp.float32)],
        compiler_params=pltpu.CompilerParams(vmem_limit_bytes=32 * 2**20),
        cost_estimate=pl.CostEstimate(
            flops=8 * SEQ * SEQ * width, bytes_accessed=8 * SEQ * width,
            transcendentals=SEQ * SEQ * heads,
        ),
        name="attention",
    )(doc_ids.reshape(tokens, 1), doc_ids.reshape(blocks, 1, SEQ), planes, planes, planes)


STEPS = (2, 1, 3, 0)


def project_kernel(place, *refs):
    acts, weights, kept, other = refs[:8], refs[8:12], refs[12], refs[13]
    a_buf, w_buf, o_buf, a_sem, w_sem, o_sem = refs[14:]
    swap, core, x_lo, y = place[0], place[1], place[2], place[3]
    depth = acts[0].shape[1]
    width = weights[0].shape[1]
    rows = acts[0].shape[0] // 8
    half = 4 * rows

    def act_copy(n, source, base, dt, dv, low, side):
        first = base + (2 * (x_lo ^ low) + (core ^ side)) * rows
        target = side * half + (2 * dt + low) * rows
        return pltpu.make_async_copy(
            source.at[pl.ds(pl.multiple_of(first, rows), rows), :],
            a_buf.at[n, pl.ds(target, rows), pl.ds(dv * depth, depth)],
            a_sem.at[n, 8 * dt + 4 * dv + 2 * low + side],
        )

    def weight_copy(dv, e):
        return pltpu.make_async_copy(
            weights[2 * dv + e],
            w_buf.at[pl.ds(pl.multiple_of((dv ^ swap) * depth, depth), depth),
                     pl.ds(pl.multiple_of((core ^ e) * width, width), width)],
            w_sem.at[dv, e],
        )

    parts = [(dt, dv, low, side) for dt in range(2) for dv in range(2)
             for low in range(2) for side in range(2)]
    pieces = [(dv, e) for dv in range(2) for e in range(2)]

    def start_acts(n):
        target = lax.rem(y + STEPS[n], 4)
        base = lax.rem(target, 2) * half
        for s in range(2):

            @pl.when(target // 2 == s)
            def _():
                for dt, dv, low, side in parts:
                    act_copy(n, acts[4 * dt + 2 * dv + s], base, dt, dv, low, side).start()

    start_acts(0)
    for piece in pieces:
        weight_copy(*piece).start()
    for piece in pieces:
        weight_copy(*piece).wait()
    for n in range(1, 4):
        start_acts(n)
    out_copies = []
    for n in range(4):
        for dt, dv, low, side in parts:
            act_copy(n, acts[0], 0, dt, dv, low, side).wait()
        for side, out in ((1, other), (0, kept)):
            product = jnp.dot(
                a_buf[n, side * half : (side + 1) * half], w_buf[...],
                preferred_element_type=jnp.float32,
            )
            o_buf[n, side] = product.astype(jnp.bfloat16)
            copy = pltpu.make_async_copy(o_buf.at[n, side], out.at[n], o_sem.at[n, side])
            copy.start()
            out_copies.append(copy)
    for copy in out_copies:
        copy.wait()


def project(place, acts, weights):
    rows, depth = acts[0].shape
    rows = rows // 2
    width = weights[0].shape[1]
    shape = (4, rows, 2 * width)
    return pl.pallas_call(
        project_kernel,
        in_specs=[pl.BlockSpec(memory_space=pltpu.SMEM)] + [pl.BlockSpec(memory_space=pl.ANY)] * 12,
        out_specs=[pl.BlockSpec(memory_space=pl.ANY)] * 2,
        out_shape=[
            jax.ShapeDtypeStruct(shape, jnp.bfloat16),
            jax.ShapeDtypeStruct(shape, jnp.bfloat16),
        ],
        scratch_shapes=[
            pltpu.VMEM((4, 2 * rows, 2 * depth), jnp.bfloat16),
            pltpu.VMEM((2 * depth, 2 * width), jnp.bfloat16),
            pltpu.VMEM((4, 2, rows, 2 * width), jnp.bfloat16),
            pltpu.SemaphoreType.DMA((4, 16)),
            pltpu.SemaphoreType.DMA((2, 2)),
            pltpu.SemaphoreType.DMA((4, 2)),
        ],
        compiler_params=pltpu.CompilerParams(vmem_limit_bytes=56 * 2**20),
        cost_estimate=pl.CostEstimate(
            flops=1, bytes_accessed=1, transcendentals=0
        ),
        name="project",
    )(place, *acts, *weights)


def pack_kernel(place, *refs):
    sources, out = refs[:8], refs[8]
    z0, core = place[1], place[2]
    width = sources[0].shape[2]
    for dg in range(2):
        for dv in range(2):
            for e in range(2):
                column = pl.multiple_of((2 * dg + (core ^ e)) * width, width)
                out[z0 ^ dv, :, :, pl.ds(column, width)] = sources[4 * dg + 2 * dv + e][...]


def pack(place, sources):
    heads, feats, width = sources[0].shape
    share = feats // 8
    return pl.pallas_call(
        pack_kernel,
        grid_spec=pltpu.PrefetchScalarGridSpec(
            num_scalar_prefetch=1,
            grid=(2,),
            in_specs=[pl.BlockSpec((heads, share, width), lambda n, place: (0, 4 * n + place[0], 0))] * 8,
            out_specs=pl.BlockSpec((2, heads, share, 4 * width), lambda n, place: (n, 0, 0, 0)),
        ),
        out_shape=jax.ShapeDtypeStruct((4, heads, share, 4 * width), jnp.bfloat16),
        compiler_params=pltpu.CompilerParams(vmem_limit_bytes=56 * 2**20),
        cost_estimate=pl.CostEstimate(
            flops=0, bytes_accessed=4 * heads * feats * width, transcendentals=0
        ),
        name="pack",
    )(place, *sources)


def columns_kernel(place, *refs):
    sources, out = refs[:8], refs[8]
    x_hi, x_lo, z1 = place[0], place[1], place[2]
    width = sources[0].shape[1] // 2
    for dg in range(2):
        for dx in range(2):
            for dl in range(2):
                for p in range(2):
                    y1, y0 = x_hi ^ (dx ^ p), z1 ^ (dg ^ p)
                    column = 8 * y1 + 4 * y0 + 2 * (x_lo ^ dl) + p
                    column = pl.multiple_of(column * width, width)
                    out[:, pl.ds(column, width)] = sources[4 * dg + 2 * dx + dl][
                        :, p * width : (p + 1) * width
                    ]


def whole_columns(place, sources, specs):
    rows, width = specs[0].block_shape[-2:]
    return pl.pallas_call(
        columns_kernel,
        grid_spec=pltpu.PrefetchScalarGridSpec(
            num_scalar_prefetch=1,
            grid=(1,),
            in_specs=specs,
            out_specs=pl.BlockSpec((rows, 8 * width), lambda r, place: (0, 0)),
        ),
        out_shape=jax.ShapeDtypeStruct((rows, 8 * width), jnp.bfloat16),
        compiler_params=pltpu.CompilerParams(vmem_limit_bytes=56 * 2**20),
        cost_estimate=pl.CostEstimate(
            flops=0, bytes_accessed=32 * rows * width, transcendentals=0
        ),
        name="columns",
    )(place, *sources)


def exchange(own, near, opposite, far):
    return [own, send(near, x_near), send(opposite, x_opposite), send(far, x_far)]


def moment_kernel(parts, out):
    count, _, _, cols = parts.shape
    for n in range(count):
        out[:, :, n * cols : (n + 1) * cols] = parts[n].astype(jnp.float32)


def moment_columns(parts):
    count, heads, feats, cols = parts.shape
    step = 4
    return pl.pallas_call(
        moment_kernel,
        grid=(count // step,),
        in_specs=[pl.BlockSpec((step, heads, feats, cols), lambda n: (n, 0, 0, 0))],
        out_specs=pl.BlockSpec((heads, feats, step * cols), lambda n: (0, 0, n)),
        out_shape=jax.ShapeDtypeStruct((heads, feats, count * cols), jnp.float32),
        compiler_params=pltpu.CompilerParams(vmem_limit_bytes=56 * 2**20),
        cost_estimate=pl.CostEstimate(
            flops=0, bytes_accessed=6 * parts.size, transcendentals=0
        ),
        name="moment_columns",
    )(parts)


def shares(total):
    total = total.reshape(4, total.shape[0] // 4, total.shape[1])
    return exchange(*[total[n] for n in range(4)])


def add_up(total, arrived):
    for part in arrived:
        total = total + part.astype(jnp.float32)
    return total.astype(jnp.bfloat16)


def tie(*values):
    return lax.optimization_barrier(values)


def local(qkv, doc_ids, old_weight, old_moment):
    x_hi, z, y, x_lo, core = (lax.axis_index(a).astype(jnp.int32) for a in AXES)
    z1, z0 = z // 2, z % 2
    ring = ("x_hi", "x_lo")
    heads, feats, cols = old_weight.shape
    heads = heads // 2

    w0 = send(lax.dynamic_slice_in_dim(old_weight, core * heads, heads, 0), spread(0))
    w1 = send(lax.dynamic_slice_in_dim(old_weight, (1 - core) * heads, heads, 0), spread(1))
    planes = qkv.transpose(1, 0, 2)
    a0 = attention(planes, doc_ids, 0)
    planes, w0, w1 = tie(planes, w0, w1)
    a1 = attention(planes, doc_ids, 1)
    near_a0, far_a0 = send(a0, x_near), send(a0, x_far)
    w0, w1, a1, near_a0, far_a0 = tie(w0, w1, a1, near_a0, far_a0)
    near_a1, far_a1 = send(a1, x_near), send(a1, x_far)
    near_w0, far_w0 = send(w0, z_near), send(w0, z_far)
    moment = old_moment.astype(jnp.bfloat16).reshape(2 * heads, 8, feats // 8, cols)
    moment = moment.transpose(1, 0, 2, 3)
    near_w0, far_w0, near_a1, far_a1, far_a0, w1, moment = tie(
        near_w0, far_w0, near_a1, far_a1, far_a0, w1, moment
    )
    opp_a0, opp_a1 = send(far_a0, x_near), send(near_a1, x_far)
    near_w1, far_w1 = send(w1, z_near), send(w1, z_far)
    near_w1, far_w1, far_w0, opp_a0, opp_a1, moment = tie(
        near_w1, far_w1, far_w0, opp_a0, opp_a1, moment
    )
    opp_w0, opp_w1 = send(far_w0, z_near), send(near_w1, z_far)
    opp_a0, opp_a1, moment = tie(opp_a0, opp_a1, moment)
    moment = lax.all_to_all(moment, ("x_hi", "z"), 0, 0, tiled=True)

    acts = [a0, a1, near_a0, near_a1, opp_a0, opp_a1, far_a0, far_a1]
    weights = ([w0, w1, near_w0, near_w1], [opp_w0, opp_w1, far_w0, far_w1])
    place = jnp.stack([x_lo ^ z0, core, x_lo, y])
    for dg in range(2):
        kept, other = project(place, acts, [w.reshape(heads * feats, cols) for w in weights[dg]])
        if dg == 0:
            other, opp_w0, opp_w1 = tie(other, opp_w0, opp_w1)
            weights = (weights[0], [opp_w0, opp_w1, far_w0, far_w1])
        else:
            kept, *packed = tie(kept, *weights[0], *weights[1])
            packed = pack(jnp.stack([z, z0, core]), packed)
            other, moment, arrived, packed = tie(other, moment, arrived, packed)
            first = add_up(total, arrived)
            packed = lax.all_to_all(packed, ("x_hi", "x_lo"), 0, 0, tiled=True)
        swapped = send(other, other_core)
        leave = [
            (kept[n].astype(jnp.float32) + swapped[n].astype(jnp.float32)).astype(jnp.bfloat16)
            for n in range(3)
        ]
        if dg == 0:
            place, *leave = tie(place, *leave)
        arrived = [send(leave[n], y_step(STEPS[n])) for n in range(3)]
        if dg == 1:
            moment, packed, arrived = tie(moment, packed, arrived)
            moment = moment.reshape(16, heads, feats // 8, cols)
            moment = lax.all_to_all(moment, ("y", "x_lo", "core"), 0, 0, tiled=True)
        total = kept[3].astype(jnp.float32) + swapped[3].astype(jnp.float32)
    total = add_up(total, arrived)
    total = jnp.stack([first, total])
    total = total.reshape(2, 4, total.shape[1] // 4, total.shape[2]).transpose(1, 0, 2, 3)
    parts = exchange(*[total[n] for n in range(4)])
    parts[1], moment = tie(parts[1], moment)
    rows, width = parts[0].shape[1:]
    specs = [
        pl.BlockSpec((None, rows, width), lambda r, place, dg=dg: (dg, 0, 0))
        for dg in range(2) for n in range(4)
    ]
    projected = whole_columns(jnp.stack([x_hi, x_lo, z1]), parts * 2, specs)

    packed = packed.reshape(4, heads * (feats // 8), 4 * cols)
    specs = [
        pl.BlockSpec((None, packed.shape[1], width), lambda r, place, dg=dg, n=n: (n, 0, dg))
        for dg in range(2) for n in range(4)
    ]
    new_weight = whole_columns(jnp.stack([0 * z1, 0 * z1, z1]), [packed] * 8, specs)
    new_weight = new_weight.reshape(heads, feats // 8, 16 * cols)
    return (new_weight, moment_columns(moment), projected)


def solution(mesh):
    mesh = Mesh(mesh.devices.reshape(SIZES), AXES)
    dp, tensor = ("x_hi", "z"), ("y", "x_lo", "core")
    placed = (P(dp, None, tensor), P(dp), P(dp, None, tensor), P(dp, None, tensor))
    return jax.shard_map(
        local,
        mesh=mesh,
        in_specs=placed,
        out_specs=(P(tensor, dp, None), P(tensor, dp, None), P(dp + tensor, None)),
        check_vma=False,
    )
```

```python
import functools

import jax
import jax.numpy as jnp
from jax import lax
from jax.experimental import pallas as pl
from jax.experimental.pallas import tpu as pltpu
from jax.sharding import Mesh, PartitionSpec as P

HEAD_DIM = 128
SEQ = 512
HALF = SEQ // 2
AXES = ("x_hi", "z", "y", "x_lo", "core")
SIZES = (2, 4, 4, 2, 2)


def pairs_of(move):
    def flat(c):
        n = 0
        for size, value in zip(SIZES, c):
            n = n * size + value
        return n

    out = []
    for x_hi in range(2):
        for z in range(4):
            for y in range(4):
                for x_lo in range(2):
                    for core in range(2):
                        here = (x_hi, z, y, x_lo, core)
                        out.append((flat(here), flat(move(*here))))
    return out


def send(value, move):
    return lax.ppermute(value, AXES, pairs_of(move))


def spread(cross):
    def move(x_hi, z, y, x_lo, core):
        x_hi, z, y = (y >> 1) ^ core, 2 * ((y & 1) ^ core) + (z & 1), 2 * x_hi + (z >> 1)
        return (x_hi, z, y, x_lo, core ^ cross)

    return move


def x_near(x_hi, z, y, x_lo, core):
    return (x_hi, z, y, 1 - x_lo, core)


def x_far(x_hi, z, y, x_lo, core):
    return (1 - x_hi, z, y, 1 - x_lo, core)


def x_opposite(x_hi, z, y, x_lo, core):
    return (1 - x_hi, z, y, x_lo, core)


def z_near(x_hi, z, y, x_lo, core):
    return (x_hi, z ^ 1, y, x_lo, core)


def z_far(x_hi, z, y, x_lo, core):
    return (x_hi, z ^ 3, y, x_lo, core)


def other_core(x_hi, z, y, x_lo, core):
    return (x_hi, z, y, x_lo, 1 - core)


def y_step(k):
    return lambda x_hi, z, y, x_lo, core: (x_hi, z, (y + k) % 4, x_lo, core)


def attention_kernel(row_doc, col_doc, q_ref, k_ref, v_ref, out_ref, bias):
    @pl.when(pl.program_id(0) == 0)
    def _():
        row = lax.broadcasted_iota(jnp.int32, (SEQ, SEQ), 0)
        col = lax.broadcasted_iota(jnp.int32, (SEQ, SEQ), 1)
        allowed = (row_doc[...] == col_doc[0]) & (row >= col)
        bias[...] = jnp.where(allowed, jnp.float32(0), jnp.float32(-1e30))

    factor = jnp.float32(HEAD_DIM**-0.5)
    for part in range(2):
        rows = slice(part * HALF, (part + 1) * HALF)
        keys = slice(0, (part + 1) * HALF)
        scores = lax.dot_general(
            q_ref[rows, :], k_ref[keys, :], (((1,), (1,)), ((), ())),
            preferred_element_type=jnp.float32,
        )
        scores = scores * factor + bias[rows, keys]
        top = jnp.max(scores, axis=-1, keepdims=True)
        expd = jnp.exp(scores - top)
        total = jnp.sum(expd, axis=-1, keepdims=True)
        mixed = jnp.dot(
            expd.astype(jnp.bfloat16), v_ref[keys, :], preferred_element_type=jnp.float32
        )
        out_ref[rows, :] = (mixed / total).astype(jnp.bfloat16)


def attention(planes, doc_ids, sequence):
    _, tokens, width = planes.shape
    heads = width // HEAD_DIM
    blocks = tokens // SEQ

    def part(n):
        return pl.BlockSpec((None, SEQ, HEAD_DIM), lambda h: (n, sequence, h))

    return pl.pallas_call(
        attention_kernel,
        grid=(heads,),
        in_specs=[
            pl.BlockSpec((SEQ, 1), lambda h: (sequence, 0)),
            pl.BlockSpec((1, 1, SEQ), lambda h: (sequence, 0, 0)),
            part(0), part(1), part(2),
        ],
        out_specs=pl.BlockSpec((SEQ, HEAD_DIM), lambda h: (0, h)),
        out_shape=jax.ShapeDtypeStruct((SEQ, width), jnp.bfloat16),
        scratch_shapes=[pltpu.VMEM((SEQ, SEQ), jnp.float32)],
        compiler_params=pltpu.CompilerParams(vmem_limit_bytes=32 * 2**20),
        cost_estimate=pl.CostEstimate(
            flops=8 * SEQ * SEQ * width, bytes_accessed=8 * SEQ * width,
            transcendentals=SEQ * SEQ * heads,
        ),
        name="attention",
    )(doc_ids.reshape(tokens, 1), doc_ids.reshape(blocks, 1, SEQ), planes, planes, planes)


STEPS = (2, 1, 3, 0)


def project_kernel(place, *refs):
    acts, weights, kept, other = refs[:8], refs[8:12], refs[12], refs[13]
    a_buf, w_buf, o_buf, a_sem, w_sem, o_sem = refs[14:]
    swap, core, x_lo, y = place[0], place[1], place[2], place[3]
    depth = acts[0].shape[1]
    width = weights[0].shape[1]
    rows = acts[0].shape[0] // 8
    half = 4 * rows

    def act_copy(n, source, base, dt, dv, low, side):
        first = base + (2 * (x_lo ^ low) + (core ^ side)) * rows
        target = side * half + (2 * dt + low) * rows
        return pltpu.make_async_copy(
            source.at[pl.ds(pl.multiple_of(first, rows), rows), :],
            a_buf.at[n, pl.ds(target, rows), pl.ds(dv * depth, depth)],
            a_sem.at[n, 8 * dt + 4 * dv + 2 * low + side],
        )

    def weight_copy(dv, e):
        return pltpu.make_async_copy(
            weights[2 * dv + e],
            w_buf.at[pl.ds(pl.multiple_of((dv ^ swap) * depth, depth), depth),
                     pl.ds(pl.multiple_of((core ^ e) * width, width), width)],
            w_sem.at[dv, e],
        )

    parts = [(dt, dv, low, side) for dt in range(2) for dv in range(2)
             for low in range(2) for side in range(2)]
    pieces = [(dv, e) for dv in range(2) for e in range(2)]

    def start_acts(n):
        target = lax.rem(y + STEPS[n], 4)
        base = lax.rem(target, 2) * half
        for s in range(2):

            @pl.when(target // 2 == s)
            def _():
                for dt, dv, low, side in parts:
                    act_copy(n, acts[4 * dt + 2 * dv + s], base, dt, dv, low, side).start()

    start_acts(0)
    for piece in pieces:
        weight_copy(*piece).start()
    for piece in pieces:
        weight_copy(*piece).wait()
    for n in range(1, 4):
        start_acts(n)
    out_copies = []
    for n in range(4):
        for dt, dv, low, side in parts:
            act_copy(n, acts[0], 0, dt, dv, low, side).wait()
        for side, out in ((1, other), (0, kept)):
            product = jnp.dot(
                a_buf[n, side * half : (side + 1) * half], w_buf[...],
                preferred_element_type=jnp.float32,
            )
            o_buf[n, side] = product.astype(jnp.bfloat16)
            copy = pltpu.make_async_copy(o_buf.at[n, side], out.at[n], o_sem.at[n, side])
            copy.start()
            out_copies.append(copy)
    for copy in out_copies:
        copy.wait()


def project(place, acts, weights):
    rows, depth = acts[0].shape
    rows = rows // 2
    width = weights[0].shape[1]
    shape = (4, rows, 2 * width)
    return pl.pallas_call(
        project_kernel,
        in_specs=[pl.BlockSpec(memory_space=pltpu.SMEM)] + [pl.BlockSpec(memory_space=pl.ANY)] * 12,
        out_specs=[pl.BlockSpec(memory_space=pl.ANY)] * 2,
        out_shape=[
            jax.ShapeDtypeStruct(shape, jnp.bfloat16),
            jax.ShapeDtypeStruct(shape, jnp.bfloat16),
        ],
        scratch_shapes=[
            pltpu.VMEM((4, 2 * rows, 2 * depth), jnp.bfloat16),
            pltpu.VMEM((2 * depth, 2 * width), jnp.bfloat16),
            pltpu.VMEM((4, 2, rows, 2 * width), jnp.bfloat16),
            pltpu.SemaphoreType.DMA((4, 16)),
            pltpu.SemaphoreType.DMA((2, 2)),
            pltpu.SemaphoreType.DMA((4, 2)),
        ],
        compiler_params=pltpu.CompilerParams(vmem_limit_bytes=56 * 2**20),
        cost_estimate=pl.CostEstimate(
            flops=1, bytes_accessed=1, transcendentals=0
        ),
        name="project",
    )(place, *acts, *weights)


def pack_kernel(place, *refs):
    sources, out = refs[:8], refs[8]
    z0, core = place[1], place[2]
    width = sources[0].shape[2]
    for dg in range(2):
        for dv in range(2):
            for e in range(2):
                column = pl.multiple_of((2 * dg + (core ^ e)) * width, width)
                out[z0 ^ dv, :, :, pl.ds(column, width)] = sources[4 * dg + 2 * dv + e][...]


def pack(place, sources):
    heads, feats, width = sources[0].shape
    share = feats // 8
    return pl.pallas_call(
        pack_kernel,
        grid_spec=pltpu.PrefetchScalarGridSpec(
            num_scalar_prefetch=1,
            grid=(2,),
            in_specs=[pl.BlockSpec((heads, share, width), lambda n, place: (0, 4 * n + place[0], 0))] * 8,
            out_specs=pl.BlockSpec((2, heads, share, 4 * width), lambda n, place: (n, 0, 0, 0)),
        ),
        out_shape=jax.ShapeDtypeStruct((4, heads, share, 4 * width), jnp.bfloat16),
        compiler_params=pltpu.CompilerParams(vmem_limit_bytes=56 * 2**20),
        cost_estimate=pl.CostEstimate(
            flops=0, bytes_accessed=4 * heads * feats * width, transcendentals=0
        ),
        name="pack",
    )(place, *sources)


def columns_kernel(place, *refs):
    sources, out = refs[:8], refs[8]
    x_hi, x_lo, z1 = place[0], place[1], place[2]
    width = sources[0].shape[1] // 2
    for dg in range(2):
        for dx in range(2):
            for dl in range(2):
                for p in range(2):
                    y1, y0 = x_hi ^ (dx ^ p), z1 ^ (dg ^ p)
                    column = 8 * y1 + 4 * y0 + 2 * (x_lo ^ dl) + p
                    column = pl.multiple_of(column * width, width)
                    out[:, pl.ds(column, width)] = sources[4 * dg + 2 * dx + dl][
                        :, p * width : (p + 1) * width
                    ]


def whole_columns(place, sources, specs):
    rows, width = specs[0].block_shape[-2:]
    return pl.pallas_call(
        columns_kernel,
        grid_spec=pltpu.PrefetchScalarGridSpec(
            num_scalar_prefetch=1,
            grid=(1,),
            in_specs=specs,
            out_specs=pl.BlockSpec((rows, 8 * width), lambda r, place: (0, 0)),
        ),
        out_shape=jax.ShapeDtypeStruct((rows, 8 * width), jnp.bfloat16),
        compiler_params=pltpu.CompilerParams(vmem_limit_bytes=56 * 2**20),
        cost_estimate=pl.CostEstimate(
            flops=0, bytes_accessed=32 * rows * width, transcendentals=0
        ),
        name="columns",
    )(place, *sources)


def moment_kernel(parts, out):
    count, _, _, cols = parts.shape
    for n in range(count):
        out[:, :, n * cols : (n + 1) * cols] = parts[n].astype(jnp.float32)


def moment_columns(parts):
    count, heads, feats, cols = parts.shape
    step = 4
    return pl.pallas_call(
        moment_kernel,
        grid=(count // step,),
        in_specs=[pl.BlockSpec((step, heads, feats, cols), lambda n: (n, 0, 0, 0))],
        out_specs=pl.BlockSpec((heads, feats, step * cols), lambda n: (0, 0, n)),
        out_shape=jax.ShapeDtypeStruct((heads, feats, count * cols), jnp.float32),
        compiler_params=pltpu.CompilerParams(vmem_limit_bytes=56 * 2**20),
        cost_estimate=pl.CostEstimate(
            flops=0, bytes_accessed=6 * parts.size, transcendentals=0
        ),
        name="moment_columns",
    )(parts)


def in_four(total):
    return total.reshape(4, total.shape[0] // 4, total.shape[1])


def add_up(total, arrived):
    for part in arrived:
        total = total + part.astype(jnp.float32)
    return total.astype(jnp.bfloat16)


def tie(*values):
    return lax.optimization_barrier(values)


def local(qkv, doc_ids, old_weight, old_moment):
    x_hi, z, y, x_lo, core = (lax.axis_index(a).astype(jnp.int32) for a in AXES)
    z1, z0 = z // 2, z % 2
    ring = ("x_hi", "x_lo")
    heads, feats, cols = old_weight.shape
    heads = heads // 2

    w0 = send(lax.dynamic_slice_in_dim(old_weight, core * heads, heads, 0), spread(0))
    w1 = send(lax.dynamic_slice_in_dim(old_weight, (1 - core) * heads, heads, 0), spread(1))
    planes = qkv.transpose(1, 0, 2)
    a0 = attention(planes, doc_ids, 0)
    planes, w0, w1 = tie(planes, w0, w1)
    a1 = attention(planes, doc_ids, 1)
    near_a0, far_a0 = send(a0, x_near), send(a0, x_far)
    w0, w1, a1, near_a0, far_a0 = tie(w0, w1, a1, near_a0, far_a0)
    near_a1, far_a1 = send(a1, x_near), send(a1, x_far)
    near_w0, far_w0 = send(w0, z_near), send(w0, z_far)
    moment = old_moment.astype(jnp.bfloat16).reshape(2 * heads, 8, feats // 8, cols)
    moment = moment.transpose(1, 0, 2, 3)
    near_w0, far_w0, near_a1, far_a1, far_a0, w1, moment = tie(
        near_w0, far_w0, near_a1, far_a1, far_a0, w1, moment
    )
    opp_a0, opp_a1 = send(far_a0, x_near), send(near_a1, x_far)
    near_w1, far_w1 = send(w1, z_near), send(w1, z_far)
    near_w1, far_w1, far_w0, opp_a0, opp_a1, moment = tie(
        near_w1, far_w1, far_w0, opp_a0, opp_a1, moment
    )
    opp_w0, opp_w1 = send(far_w0, z_near), send(near_w1, z_far)
    opp_a0, opp_a1, moment = tie(opp_a0, opp_a1, moment)
    moment = lax.all_to_all(moment, ("x_hi", "z"), 0, 0, tiled=True)

    acts = [a0, a1, near_a0, near_a1, opp_a0, opp_a1, far_a0, far_a1]
    weights = ([w0, w1, near_w0, near_w1], [opp_w0, opp_w1, far_w0, far_w1])
    place = jnp.stack([x_lo ^ z0, core, x_lo, y])
    for dg in range(2):
        kept, other = project(place, acts, [w.reshape(heads * feats, cols) for w in weights[dg]])
        if dg == 0:
            other, opp_w0, opp_w1 = tie(other, opp_w0, opp_w1)
            weights = (weights[0], [opp_w0, opp_w1, far_w0, far_w1])
        else:
            kept, *packed = tie(kept, *weights[0], *weights[1])
            packed = pack(jnp.stack([z, z0, core]), packed)
            other, moment, arrived, packed = tie(other, moment, arrived, packed)
            first = in_four(add_up(total, arrived))
            early = [send(first[1], x_near), send(first[2], x_opposite)]
            packed = lax.all_to_all(packed, ("x_hi", "x_lo"), 0, 0, tiled=True)
        swapped = send(other, other_core)
        leave = [
            (kept[n].astype(jnp.float32) + swapped[n].astype(jnp.float32)).astype(jnp.bfloat16)
            for n in range(3)
        ]
        if dg == 0:
            place, *leave = tie(place, *leave)
        arrived = [send(leave[n], y_step(STEPS[n])) for n in range(3)]
        if dg == 1:
            moment, packed, arrived, early = tie(moment, packed, arrived, early)
            moment = moment.reshape(16, heads, feats // 8, cols)
            moment = lax.all_to_all(moment, ("y", "x_lo", "core"), 0, 0, tiled=True)
        total = kept[3].astype(jnp.float32) + swapped[3].astype(jnp.float32)
    total = in_four(add_up(total, arrived))
    far = send(jnp.stack([first[3], total[3]]), x_far)
    rows, width = total.shape[1:]
    parts = [first[0], *early, far, total[0], send(total[1], x_near), send(total[2], x_opposite), far]
    whole = pl.BlockSpec((rows, width), lambda r, place: (0, 0))
    half = [pl.BlockSpec((None, rows, width), lambda r, place, dg=dg: (dg, 0, 0)) for dg in range(2)]
    specs = [whole] * 3 + [half[0]] + [whole] * 3 + [half[1]]
    projected = whole_columns(jnp.stack([x_hi, x_lo, z1]), parts, specs)

    packed = packed.reshape(4, heads * (feats // 8), 4 * cols)
    specs = [
        pl.BlockSpec((None, packed.shape[1], width), lambda r, place, dg=dg, n=n: (n, 0, dg))
        for dg in range(2) for n in range(4)
    ]
    new_weight = whole_columns(jnp.stack([0 * z1, 0 * z1, z1]), [packed] * 8, specs)
    new_weight = new_weight.reshape(heads, feats // 8, 16 * cols)
    return (new_weight, moment_columns(moment), projected)


def solution(mesh):
    mesh = Mesh(mesh.devices.reshape(SIZES), AXES)
    dp, tensor = ("x_hi", "z"), ("y", "x_lo", "core")
    placed = (P(dp, None, tensor), P(dp), P(dp, None, tensor), P(dp, None, tensor))
    return jax.shard_map(
        local,
        mesh=mesh,
        in_specs=placed,
        out_specs=(P(tensor, dp, None), P(tensor, dp, None), P(dp + tensor, None)),
        check_vma=False,
    )
```

```python
import functools

import jax
import jax.numpy as jnp
from jax import lax
from jax.experimental import pallas as pl
from jax.experimental.pallas import tpu as pltpu
from jax.sharding import Mesh, PartitionSpec as P

HEAD_DIM = 128
SEQ = 512
HALF = SEQ // 2
AXES = ("x_hi", "z", "y", "x_lo", "core")
SIZES = (2, 4, 4, 2, 2)


def pairs_of(move):
    def flat(c):
        n = 0
        for size, value in zip(SIZES, c):
            n = n * size + value
        return n

    out = []
    for x_hi in range(2):
        for z in range(4):
            for y in range(4):
                for x_lo in range(2):
                    for core in range(2):
                        here = (x_hi, z, y, x_lo, core)
                        out.append((flat(here), flat(move(*here))))
    return out


def send(value, move):
    return lax.ppermute(value, AXES, pairs_of(move))


def spread(cross):
    def move(x_hi, z, y, x_lo, core):
        x_hi, z, y = (y >> 1) ^ core, 2 * ((y & 1) ^ core) + (z & 1), 2 * x_hi + (z >> 1)
        return (x_hi, z, y, x_lo, core ^ cross)

    return move


def x_near(x_hi, z, y, x_lo, core):
    return (x_hi, z, y, 1 - x_lo, core)


def x_far(x_hi, z, y, x_lo, core):
    return (1 - x_hi, z, y, 1 - x_lo, core)


def x_opposite(x_hi, z, y, x_lo, core):
    return (1 - x_hi, z, y, x_lo, core)


def z_near(x_hi, z, y, x_lo, core):
    return (x_hi, z ^ 1, y, x_lo, core)


def z_far(x_hi, z, y, x_lo, core):
    return (x_hi, z ^ 3, y, x_lo, core)


def other_core(x_hi, z, y, x_lo, core):
    return (x_hi, z, y, x_lo, 1 - core)


def y_step(k):
    return lambda x_hi, z, y, x_lo, core: (x_hi, z, (y + k) % 4, x_lo, core)


def attention_kernel(row_doc, col_doc, q_ref, k_ref, v_ref, out_ref, bias):
    @pl.when(pl.program_id(0) == 0)
    def _():
        row = lax.broadcasted_iota(jnp.int32, (SEQ, SEQ), 0)
        col = lax.broadcasted_iota(jnp.int32, (SEQ, SEQ), 1)
        allowed = (row_doc[...] == col_doc[0]) & (row >= col)
        bias[...] = jnp.where(allowed, jnp.float32(0), jnp.float32(-1e30))

    factor = jnp.float32(HEAD_DIM**-0.5)
    for part in range(2):
        rows = slice(part * HALF, (part + 1) * HALF)
        keys = slice(0, (part + 1) * HALF)
        scores = lax.dot_general(
            q_ref[rows, :], k_ref[keys, :], (((1,), (1,)), ((), ())),
            preferred_element_type=jnp.float32,
        )
        scores = scores * factor + bias[rows, keys]
        top = jnp.max(scores, axis=-1, keepdims=True)
        expd = jnp.exp(scores - top)
        total = jnp.sum(expd, axis=-1, keepdims=True)
        mixed = jnp.dot(
            expd.astype(jnp.bfloat16), v_ref[keys, :], preferred_element_type=jnp.float32
        )
        out_ref[rows, :] = (mixed / total).astype(jnp.bfloat16)


def attention(planes, doc_ids, sequence):
    _, tokens, width = planes.shape
    heads = width // HEAD_DIM
    blocks = tokens // SEQ

    def part(n):
        return pl.BlockSpec((None, SEQ, HEAD_DIM), lambda h: (n, sequence, h))

    return pl.pallas_call(
        attention_kernel,
        grid=(heads,),
        in_specs=[
            pl.BlockSpec((SEQ, 1), lambda h: (sequence, 0)),
            pl.BlockSpec((1, 1, SEQ), lambda h: (sequence, 0, 0)),
            part(0), part(1), part(2),
        ],
        out_specs=pl.BlockSpec((SEQ, HEAD_DIM), lambda h: (0, h)),
        out_shape=jax.ShapeDtypeStruct((SEQ, width), jnp.bfloat16),
        scratch_shapes=[pltpu.VMEM((SEQ, SEQ), jnp.float32)],
        compiler_params=pltpu.CompilerParams(vmem_limit_bytes=32 * 2**20),
        cost_estimate=pl.CostEstimate(
            flops=8 * SEQ * SEQ * width, bytes_accessed=8 * SEQ * width,
            transcendentals=SEQ * SEQ * heads,
        ),
        name="attention",
    )(doc_ids.reshape(tokens, 1), doc_ids.reshape(blocks, 1, SEQ), planes, planes, planes)


STEPS = (2, 1, 3, 0)


def project_kernel(place, *refs):
    acts, weights, kept, other = refs[:8], refs[8:12], refs[12], refs[13]
    a_buf, w_buf, o_buf, a_sem, w_sem, o_sem = refs[14:]
    swap, core, x_lo, y = place[0], place[1], place[2], place[3]
    depth = acts[0].shape[1]
    width = weights[0].shape[1]
    rows = acts[0].shape[0] // 8
    half = 4 * rows

    def act_copy(n, source, base, dt, dv, low, side):
        first = base + (2 * (x_lo ^ low) + (core ^ side)) * rows
        target = side * half + (2 * dt + low) * rows
        return pltpu.make_async_copy(
            source.at[pl.ds(pl.multiple_of(first, rows), rows), :],
            a_buf.at[n, pl.ds(target, rows), pl.ds(dv * depth, depth)],
            a_sem.at[n, 8 * dt + 4 * dv + 2 * low + side],
        )

    def weight_copy(dv, e):
        return pltpu.make_async_copy(
            weights[2 * dv + e],
            w_buf.at[pl.ds(pl.multiple_of((dv ^ swap) * depth, depth), depth),
                     pl.ds(pl.multiple_of((core ^ e) * width, width), width)],
            w_sem.at[dv, e],
        )

    parts = [(dt, dv, low, side) for dt in range(2) for dv in range(2)
             for low in range(2) for side in range(2)]
    pieces = [(dv, e) for dv in range(2) for e in range(2)]

    def start_acts(n):
        target = lax.rem(y + STEPS[n], 4)
        base = lax.rem(target, 2) * half
        for s in range(2):

            @pl.when(target // 2 == s)
            def _():
                for dt, dv, low, side in parts:
                    act_copy(n, acts[4 * dt + 2 * dv + s], base, dt, dv, low, side).start()

    start_acts(0)
    for piece in pieces:
        weight_copy(*piece).start()
    for piece in pieces:
        weight_copy(*piece).wait()
    for n in range(1, 4):
        start_acts(n)
    out_copies = []
    for n in range(4):
        for dt, dv, low, side in parts:
            act_copy(n, acts[0], 0, dt, dv, low, side).wait()
        for side, out in ((1, other), (0, kept)):
            product = jnp.dot(
                a_buf[n, side * half : (side + 1) * half], w_buf[...],
                preferred_element_type=jnp.float32,
            )
            o_buf[n, side] = product.astype(jnp.bfloat16)
            copy = pltpu.make_async_copy(o_buf.at[n, side], out.at[n], o_sem.at[n, side])
            copy.start()
            out_copies.append(copy)
    for copy in out_copies:
        copy.wait()


def project(place, acts, weights):
    rows, depth = acts[0].shape
    rows = rows // 2
    width = weights[0].shape[1]
    shape = (4, rows, 2 * width)
    return pl.pallas_call(
        project_kernel,
        in_specs=[pl.BlockSpec(memory_space=pltpu.SMEM)] + [pl.BlockSpec(memory_space=pl.ANY)] * 12,
        out_specs=[pl.BlockSpec(memory_space=pl.ANY)] * 2,
        out_shape=[
            jax.ShapeDtypeStruct(shape, jnp.bfloat16),
            jax.ShapeDtypeStruct(shape, jnp.bfloat16),
        ],
        scratch_shapes=[
            pltpu.VMEM((4, 2 * rows, 2 * depth), jnp.bfloat16),
            pltpu.VMEM((2 * depth, 2 * width), jnp.bfloat16),
            pltpu.VMEM((4, 2, rows, 2 * width), jnp.bfloat16),
            pltpu.SemaphoreType.DMA((4, 16)),
            pltpu.SemaphoreType.DMA((2, 2)),
            pltpu.SemaphoreType.DMA((4, 2)),
        ],
        compiler_params=pltpu.CompilerParams(vmem_limit_bytes=56 * 2**20),
        cost_estimate=pl.CostEstimate(
            flops=1, bytes_accessed=1, transcendentals=0
        ),
        name="project",
    )(place, *acts, *weights)


def pack_kernel(place, *refs):
    sources, out = refs[:8], refs[8]
    z0, core = place[1], place[2]
    width = sources[0].shape[2]
    for dg in range(2):
        for dv in range(2):
            for e in range(2):
                column = pl.multiple_of((2 * dg + (core ^ e)) * width, width)
                out[z0 ^ dv, :, :, pl.ds(column, width)] = sources[4 * dg + 2 * dv + e][...]


def pack(place, sources):
    heads, feats, width = sources[0].shape
    share = feats // 8
    return pl.pallas_call(
        pack_kernel,
        grid_spec=pltpu.PrefetchScalarGridSpec(
            num_scalar_prefetch=1,
            grid=(2,),
            in_specs=[pl.BlockSpec((heads, share, width), lambda n, place: (0, 4 * n + place[0], 0))] * 8,
            out_specs=pl.BlockSpec((2, heads, share, 4 * width), lambda n, place: (n, 0, 0, 0)),
        ),
        out_shape=jax.ShapeDtypeStruct((4, heads, share, 4 * width), jnp.bfloat16),
        compiler_params=pltpu.CompilerParams(vmem_limit_bytes=56 * 2**20),
        cost_estimate=pl.CostEstimate(
            flops=0, bytes_accessed=4 * heads * feats * width, transcendentals=0
        ),
        name="pack",
    )(place, *sources)


def columns_kernel(place, *refs):
    sources, out = refs[:8], refs[8]
    x_hi, x_lo, z1 = place[0], place[1], place[2]
    width = sources[0].shape[1] // 2
    for dg in range(2):
        for dx in range(2):
            for dl in range(2):
                for p in range(2):
                    y1, y0 = x_hi ^ (dx ^ p), z1 ^ (dg ^ p)
                    column = 8 * y1 + 4 * y0 + 2 * (x_lo ^ dl) + p
                    column = pl.multiple_of(column * width, width)
                    out[:, pl.ds(column, width)] = sources[4 * dg + 2 * dx + dl][
                        :, p * width : (p + 1) * width
                    ]


def whole_columns(place, sources, specs):
    rows, width = specs[0].block_shape[-2:]
    return pl.pallas_call(
        columns_kernel,
        grid_spec=pltpu.PrefetchScalarGridSpec(
            num_scalar_prefetch=1,
            grid=(1,),
            in_specs=specs,
            out_specs=pl.BlockSpec((rows, 8 * width), lambda r, place: (0, 0)),
        ),
        out_shape=jax.ShapeDtypeStruct((rows, 8 * width), jnp.bfloat16),
        compiler_params=pltpu.CompilerParams(vmem_limit_bytes=56 * 2**20),
        cost_estimate=pl.CostEstimate(
            flops=0, bytes_accessed=32 * rows * width, transcendentals=0
        ),
        name="columns",
    )(place, *sources)


def moment_kernel(parts, out):
    count, _, _, cols = parts.shape
    for n in range(count):
        out[:, :, n * cols : (n + 1) * cols] = parts[n].astype(jnp.float32)


def moment_columns(parts):
    count, heads, feats, cols = parts.shape
    step = 2
    return pl.pallas_call(
        moment_kernel,
        grid=(count // step,),
        in_specs=[pl.BlockSpec((step, heads, feats, cols), lambda n: (n, 0, 0, 0))],
        out_specs=pl.BlockSpec((heads, feats, step * cols), lambda n: (0, 0, n)),
        out_shape=jax.ShapeDtypeStruct((heads, feats, count * cols), jnp.float32),
        compiler_params=pltpu.CompilerParams(vmem_limit_bytes=56 * 2**20),
        cost_estimate=pl.CostEstimate(
            flops=0, bytes_accessed=6 * parts.size, transcendentals=0
        ),
        name="moment_columns",
    )(parts)


def in_four(total):
    return total.reshape(4, total.shape[0] // 4, total.shape[1])


def add_up(total, arrived):
    for part in arrived:
        total = total + part.astype(jnp.float32)
    return total.astype(jnp.bfloat16)


def tie(*values):
    return lax.optimization_barrier(values)


def local(qkv, doc_ids, old_weight, old_moment):
    x_hi, z, y, x_lo, core = (lax.axis_index(a).astype(jnp.int32) for a in AXES)
    z1, z0 = z // 2, z % 2
    ring = ("x_hi", "x_lo")
    heads, feats, cols = old_weight.shape
    heads = heads // 2

    w0 = send(lax.dynamic_slice_in_dim(old_weight, core * heads, heads, 0), spread(0))
    w1 = send(lax.dynamic_slice_in_dim(old_weight, (1 - core) * heads, heads, 0), spread(1))
    planes = qkv.transpose(1, 0, 2)
    a0 = attention(planes, doc_ids, 0)
    planes, w0, w1 = tie(planes, w0, w1)
    a1 = attention(planes, doc_ids, 1)
    near_a0, far_a0 = send(a0, x_near), send(a0, x_far)
    a1, near_a0, far_a0 = tie(a1, near_a0, far_a0)
    near_a1, far_a1 = send(a1, x_near), send(a1, x_far)
    near_w0, far_w0 = send(w0, z_near), send(w0, z_far)
    moment = old_moment.astype(jnp.bfloat16).reshape(2 * heads, 8, feats // 8, cols)
    moment = moment.transpose(1, 0, 2, 3)
    near_w0, far_w0, near_a1, far_a1, far_a0, w1, moment = tie(
        near_w0, far_w0, near_a1, far_a1, far_a0, w1, moment
    )
    opp_a0, opp_a1 = send(far_a0, x_near), send(near_a1, x_far)
    near_w1, far_w1 = send(w1, z_near), send(w1, z_far)
    near_w1, far_w1, far_w0, opp_a0, opp_a1, moment = tie(
        near_w1, far_w1, far_w0, opp_a0, opp_a1, moment
    )
    opp_w0, opp_w1 = send(far_w0, z_near), send(near_w1, z_far)
    opp_a0, opp_a1, moment = tie(opp_a0, opp_a1, moment)
    moment = lax.all_to_all(moment, ("x_hi", "z"), 0, 0, tiled=True)

    acts = [a0, a1, near_a0, near_a1, opp_a0, opp_a1, far_a0, far_a1]
    weights = ([w0, w1, near_w0, near_w1], [opp_w0, opp_w1, far_w0, far_w1])
    place = jnp.stack([x_lo ^ z0, core, x_lo, y])
    for dg in range(2):
        kept, other = project(place, acts, [w.reshape(heads * feats, cols) for w in weights[dg]])
        if dg == 0:
            other, opp_w0, opp_w1 = tie(other, opp_w0, opp_w1)
            weights = (weights[0], [opp_w0, opp_w1, far_w0, far_w1])
        else:
            kept, *packed = tie(kept, *weights[0], *weights[1])
            packed = pack(jnp.stack([z, z0, core]), packed)
            other, moment, arrived, packed = tie(other, moment, arrived, packed)
            first = in_four(add_up(total, arrived))
            early = [send(first[1], x_near), send(first[2], x_opposite)]
            packed = lax.all_to_all(packed, ("x_hi", "x_lo"), 0, 0, tiled=True)
        swapped = send(other, other_core)
        leave = [
            (kept[n].astype(jnp.float32) + swapped[n].astype(jnp.float32)).astype(jnp.bfloat16)
            for n in range(3)
        ]
        if dg == 0:
            place, *leave = tie(place, *leave)
        arrived = [send(leave[n], y_step(STEPS[n])) for n in range(3)]
        if dg == 1:
            moment, packed, arrived, early = tie(moment, packed, arrived, early)
            moment = moment.reshape(16, heads, feats // 8, cols)
            moment = lax.all_to_all(moment, ("y", "x_lo", "core"), 0, 0, tiled=True)
        total = kept[3].astype(jnp.float32) + swapped[3].astype(jnp.float32)
    total = in_four(add_up(total, arrived))
    far = send(jnp.stack([first[3], total[3]]), x_far)
    rows, width = total.shape[1:]
    parts = [first[0], *early, far, total[0], send(total[1], x_near), send(total[2], x_opposite), far]
    whole = pl.BlockSpec((rows, width), lambda r, place: (0, 0))
    half = [pl.BlockSpec((None, rows, width), lambda r, place, dg=dg: (dg, 0, 0)) for dg in range(2)]
    specs = [whole] * 3 + [half[0]] + [whole] * 3 + [half[1]]
    projected = whole_columns(jnp.stack([x_hi, x_lo, z1]), parts, specs)

    packed = packed.reshape(4, heads * (feats // 8), 4 * cols)
    specs = [
        pl.BlockSpec((None, packed.shape[1], width), lambda r, place, dg=dg, n=n: (n, 0, dg))
        for dg in range(2) for n in range(4)
    ]
    new_weight = whole_columns(jnp.stack([0 * z1, 0 * z1, z1]), [packed] * 8, specs)
    new_weight = new_weight.reshape(heads, feats // 8, 16 * cols)
    return (new_weight, moment_columns(moment), projected)


def solution(mesh):
    mesh = Mesh(mesh.devices.reshape(SIZES), AXES)
    dp, tensor = ("x_hi", "z"), ("y", "x_lo", "core")
    placed = (P(dp, None, tensor), P(dp), P(dp, None, tensor), P(dp, None, tensor))
    return jax.shard_map(
        local,
        mesh=mesh,
        in_specs=placed,
        out_specs=(P(tensor, dp, None), P(tensor, dp, None), P(dp + tensor, None)),
        check_vma=False,
    )
```
